32 devices in a mesh: groups: 2 (over y), row: 4 (over z), col: 4 (over x, core).
Axes of the slice: x: 2, y: 2, z: 4, core: 2. Of those that a mesh axis runs over, the one named last changes fastest.
Arguments:
- values: float32 [1024, 4, 128, 128], P(('groups', 'row'), 'col'), parts along dimension 0, as said below
- partner: int32 [1024, 4], P(('groups', 'row'), 'col'), parts along dimension 0, may hold values from 0 to 511, as said below
Outputs:
- product: float32 [1024, 4, 128, 128], P(('groups', 'row'), 'col'), parts along dimension 0
The draws below stay inside these ranges and needn't reach their ends.
There are 2 independent parts, one for each index of `groups`. The reference program is written for one: setup_inputs(seed, part) draws one part's arguments, and reference() takes and returns one part's arrays. A program takes and returns all parts, laid end to end along the dimension named above; each array names one. Nothing has to cross between parts.
Inputs may be any that keep to these rules, and one draw needn't show every extreme that they name: partner[i, c] lies in column range c, that is c * 128 <= partner[i, c] < (c + 1) * 128; partner[i, i // 128] = i; the pattern is symmetric: partner[partner[i, c], i // 128] = i. values[i, c] is the transpose of values[partner[i, c], i // 128], so X is symmetric.
All inputs are finite; a program needn't handle non-finite values.
Results may differ from the reference program's by a relative error of at most 0.0003.
Values sent between devices are 32-bit elements; how exact they have to be, the bound alone decides.
A program may use at most 192 MiB of HBM per device.

```python
import math
import jax
import jax.numpy as jnp
from jax import lax

NB = 512
BLK = 128
STEPS = 3
SLOTS = 4
RANGE = 128


def build_pattern(key):
    key = jax.random.fold_in(key, 11)
    keys = jax.random.split(key, 3)
    labels = jax.vmap(lambda single: jax.random.permutation(single, RANGE))(jax.random.split(keys[0], SLOTS)).astype(jnp.int32)
    inverse_labels = jnp.argsort(labels, axis=1, stable=True).astype(jnp.int32)
    shuffles = jax.vmap(lambda single: jax.random.permutation(single, RANGE))(jax.random.split(keys[1], SLOTS * SLOTS)).astype(jnp.int32)
    shuffles = shuffles.reshape(SLOTS, SLOTS, RANGE)
    shuffles_inverse = jnp.argsort(shuffles, axis=2, stable=True).astype(jnp.int32)
    coin_flips = jax.random.randint(keys[2], (SLOTS, SLOTS), 0, 4)
    row_ranges = jnp.arange(SLOTS, dtype=jnp.int32)[:, None]
    col_ranges = jnp.arange(SLOTS, dtype=jnp.int32)[None, :]
    lower_range = jnp.minimum(row_ranges, col_ranges)
    upper_range = jnp.maximum(row_ranges, col_ranges)
    defects = (coin_flips[lower_range, upper_range] == 0) & (row_ranges != col_ranges)
    own_labels = jnp.broadcast_to(labels[:, None, :], (SLOTS, SLOTS, RANGE))
    target_ranges = jnp.broadcast_to(col_ranges[:, :, None], (SLOTS, SLOTS, RANGE))
    consistent = inverse_labels[target_ranges, own_labels]
    scrambled = jnp.where((row_ranges < col_ranges)[:, :, None], shuffles, jnp.transpose(shuffles_inverse, (1, 0, 2)))
    mapping = jnp.where(defects[:, :, None], scrambled, consistent)
    partner = jnp.transpose(mapping, (0, 2, 1)).reshape(NB, SLOTS) + jnp.arange(SLOTS, dtype=jnp.int32)[None, :] * RANGE
    return partner.astype(jnp.int32)


def draw_partner(key, part):
    return build_pattern(key)


def draw_values(key, part):
    partner = build_pattern(key)
    key = jax.random.fold_in(key, 5)
    raw_blocks = 0.3 * jax.random.normal(key, (NB, SLOTS, BLK, BLK), jnp.float32)
    own_range = (jnp.arange(NB, dtype=jnp.int32) // RANGE)[:, None]
    mirrored = raw_blocks[partner, own_range]
    return (raw_blocks + jnp.swapaxes(mirrored, 2, 3)) * (1.0 / math.sqrt(2.0))


def setup_inputs(seed: int = 0, part: int = 0) -> dict:
    streams_of = jax.random.split(jax.random.key(seed), 3)
    part_keys = jax.random.split(jax.random.fold_in(streams_of[2], part), 3)
    return {
        "values": draw_values(jax.random.fold_in(jax.random.fold_in(streams_of[2], part), 71), part),
        "partner": draw_partner(jax.random.fold_in(jax.random.fold_in(streams_of[2], part), 71), part),
    }


def reference(values, partner):
    slot_count = partner.shape[1]
    columns = jnp.arange(slot_count, dtype=jnp.int32)

    def add_range(accumulated, window):
        forward = ((columns + window) % slot_count).astype(jnp.int32)
        between = partner[:, forward]
        left_blocks = values[:, forward]
        right_blocks = values[between, columns[None, :]]
        reached = partner[between, columns[None, :]]
        product = jnp.einsum("ncxy,ncyz->ncxz", left_blocks, right_blocks, precision=lax.Precision.HIGHEST)
        matches = (reached == partner)[:, :, None, None]
        return accumulated + jnp.where(matches, product, 0.0), None

    accumulated, _ = lax.scan(add_range, jnp.zeros(values.shape, jnp.float32), jnp.arange(STEPS, dtype=jnp.int32))
    return accumulated
```

```python
import functools
import jax
import jax.numpy as jnp
from jax import lax
from jax.experimental import pallas as pl
from jax.experimental.pallas import tpu as pltpu
from jax.sharding import PartitionSpec as P

STEPS = 3
MESH = pl.DeviceIdType.MESH
SIDE = 4
CHUNKS = 8
GROUP = 4

FLOWS = (
    (0, 0, 0, 1, 0, 1, 0),
    (0, 0, 0, 2, 0, 1, 1),
    (0, 1, 0, 2, 0, 2, 0),
    (0, 1, 0, 3, 0, 3, 0),
    (0, 1, 1, 1, 1, 1, 0),
    (0, 1, 1, 2, 1, 1, 1),
    (0, 1, 3, 1, 2, 1, 1),
    (0, 2, 0, 3, 0, 3, 0),
    (0, 2, 0, 0, 0, 0, 0),
    (0, 2, 2, 2, 1, 2, 1),
    (0, 2, 2, 3, 1, 2, 1),
    (0, 3, 0, 0, 0, 2, 1),
    (0, 3, 0, 1, 0, 1, 0),
    (0, 3, 3, 3, 1, 3, 2),
    (0, 3, 3, 1, 0, 1, 2),
    (1, 0, 1, 1, 1, 1, 0),
    (1, 0, 1, 2, 1, 1, 1),
    (1, 0, 0, 0, 0, 0, 0),
    (1, 0, 2, 0, 2, 0, 0),
    (1, 1, 1, 2, 1, 2, 0),
    (1, 1, 1, 3, 1, 2, 1),
    (1, 2, 1, 3, 1, 3, 0),
    (1, 2, 1, 0, 1, 0, 0),
    (1, 2, 2, 2, 2, 2, 0),
    (1, 2, 2, 3, 2, 3, 0),
    (1, 2, 0, 2, 0, 2, 0),
    (1, 3, 1, 0, 1, 2, 1),
    (1, 3, 1, 1, 1, 1, 0),
    (1, 3, 3, 3, 2, 3, 1),
    (1, 3, 0, 3, 0, 2, 1),
    (2, 0, 2, 1, 2, 1, 0),
    (2, 0, 2, 2, 2, 1, 1),
    (2, 0, 0, 0, 1, 0, 1),
    (2, 0, 0, 1, 3, 0, 1),
    (2, 1, 2, 2, 2, 2, 0),
    (2, 1, 2, 3, 2, 3, 0),
    (2, 1, 1, 1, 1, 0, 1),
    (2, 1, 3, 1, 3, 1, 0),
    (2, 2, 2, 3, 2, 3, 0),
    (2, 2, 2, 0, 2, 3, 1),
    (2, 3, 2, 0, 2, 0, 0),
    (2, 3, 2, 1, 2, 1, 0),
    (2, 3, 3, 3, 3, 3, 0),
    (2, 3, 3, 0, 3, 2, 2),
    (2, 3, 1, 3, 1, 3, 0),
    (3, 0, 3, 1, 3, 1, 0),
    (3, 0, 3, 2, 3, 1, 1),
    (3, 0, 0, 0, 2, 0, 2),
    (3, 0, 0, 1, 0, 1, 0),
    (3, 0, 2, 0, 3, 2, 2),
    (3, 1, 3, 2, 3, 2, 0),
    (3, 1, 3, 3, 3, 3, 0),
    (3, 1, 1, 1, 2, 1, 2),
    (3, 1, 2, 1, 2, 1, 0),
    (3, 2, 3, 3, 3, 3, 0),
    (3, 2, 3, 0, 3, 3, 1),
    (3, 2, 2, 2, 2, 2, 0),
    (3, 2, 2, 0, 2, 3, 1),
    (3, 3, 3, 0, 3, 0, 0),
    (3, 3, 3, 1, 3, 1, 0),
)


def plan():
    devices = [(r, c) for r in range(SIDE) for c in range(SIDE)]
    forwarded = {(s, p) for _, p, s, _ in split_flows() if s != p}
    slots = {}
    for device in devices:
        arriving = [(p, hops) for d, p, _, hops in split_flows() if d == device]
        arriving.sort(key=lambda item: ((device, item[0]) not in forwarded, item[1]))
        slots[device] = {device: 0}
        for slot, (panel, _) in enumerate(arriving):
            slots[device][panel] = slot + 1
    slot_count = max(len(held) for held in slots.values())
    sends = {device: [] for device in devices}
    forwards = {device: [[] for _ in range(slot_count)] for device in devices}
    senders = {device: [None] * slot_count for device in devices}
    for receiver, panel, sender, _ in split_flows():
        target = (slots[receiver][panel], receiver)
        senders[receiver][target[0]] = sender
        if sender == panel:
            sends[sender].append(target)
        else:
            forwards[sender][slots[sender][panel]].append(target)
    return devices, slots, slot_count, sends, forwards, senders


def split_flows():
    return [((a, b), (c, d), (e, f), hops) for a, b, c, d, e, f, hops in FLOWS]


def encoded(target):
    return -1 if target is None else (target[0] * SIDE + target[1][0]) * SIDE + target[1][1]


def picked(me, table):
    value = jnp.int32(table[0])
    for position in range(1, len(table)):
        if table[position] != table[0]:
            value = jnp.where(me == position, jnp.int32(table[position]), value)
    return value


def padded(items, count):
    return list(items) + [None] * (count - len(items))


def transport_kernel(own_ref, held_ref, send_sem, recv_sem, own_sem):
    devices, _, slot_count, sends, forwards, senders = plan()
    group, row, col = lax.axis_index("groups"), lax.axis_index("row"), lax.axis_index("col")
    me = row * SIDE + col
    send_count = max(len(sends[d]) for d in devices)
    fan = [max(len(forwards[d][slot]) for d in devices) for slot in range(slot_count)]
    chunk = own_ref.shape[0] // CHUNKS

    def table(entry):
        return picked(me, [encoded(entry(d)) for d in devices])

    send_codes = [table(lambda d: padded(sends[d], send_count)[k]) for k in range(send_count)]
    forward_codes = [
        [table(lambda d: padded(forwards[d][slot], fan[slot])[k]) for k in range(fan[slot])]
        for slot in range(slot_count)
    ]
    sender_codes = [
        table(lambda d: None if senders[d][slot] is None else (0, senders[d][slot]))
        for slot in range(slot_count)
    ]
    all_codes = send_codes + [code for codes in forward_codes for code in codes]

    def place(code):
        return (group, code // SIDE % SIDE, code % SIDE)

    barrier = pltpu.get_barrier_semaphore()
    for slot in range(1, slot_count):
        @pl.when(sender_codes[slot] >= 0)
        def _():
            pl.semaphore_signal(
                barrier, inc=1, device_id=place(sender_codes[slot]), device_id_type=MESH
            )
    receivers = [len(sends[d]) + sum(len(targets) for targets in forwards[d]) for d in devices]
    pl.semaphore_wait(barrier, picked(me, receivers))

    own_copy = pltpu.make_async_copy(own_ref, held_ref.at[0], own_sem)

    def piece(q):
        return pl.ds(q * chunk, chunk)

    def moved(source, code, index, q):
        slot = code // (SIDE * SIDE)
        return pltpu.make_async_remote_copy(
            src_ref=source,
            dst_ref=held_ref.at[slot, piece(q)],
            send_sem=send_sem.at[index, q],
            recv_sem=recv_sem.at[slot, q],
            device_id=place(code),
            device_id_type=MESH,
        )

    def arrived(slot, q):
        pltpu.make_async_remote_copy(
            src_ref=held_ref.at[slot, piece(q)],
            dst_ref=held_ref.at[slot, piece(q)],
            send_sem=send_sem.at[0, q],
            recv_sem=recv_sem.at[slot, q],
            device_id=place(sender_codes[slot]),
            device_id_type=MESH,
        ).wait_recv()

    def start_own(q, carry):
        for index, code in enumerate(send_codes):
            @pl.when(code >= 0)
            def _():
                moved(own_ref.at[piece(q)], code, index, q).start()
        return carry

    lax.fori_loop(0, CHUNKS, start_own, 0)
    own_copy.start()

    def pass_on(q, carry):
        index = send_count
        for slot in range(1, slot_count):
            if not fan[slot]:
                continue

            @pl.when(forward_codes[slot][0] >= 0)
            def _():
                arrived(slot, q)
            for code in forward_codes[slot]:
                @pl.when(code >= 0)
                def _():
                    moved(held_ref.at[slot, piece(q)], code, index, q).start()
                index += 1
        return carry

    lax.fori_loop(0, CHUNKS, pass_on, 0)

    def finish(q, carry):
        for slot in range(1, slot_count):
            waits = sender_codes[slot] >= 0
            if fan[slot]:
                waits = jnp.logical_and(waits, forward_codes[slot][0] < 0)

            @pl.when(waits)
            def _():
                arrived(slot, q)
        for index, code in enumerate(all_codes):
            @pl.when(code >= 0)
            def _():
                moved(own_ref.at[piece(q)], code, index, q).wait_send()
        return carry

    lax.fori_loop(0, CHUNKS, finish, 0)
    own_copy.wait()


def transported(own_block):
    devices, _, slot_count, sends, forwards, _ = plan()
    copies = max(len(sends[d]) for d in devices) + sum(
        max(len(forwards[d][slot]) for d in devices) for slot in range(slot_count)
    )
    return pl.pallas_call(
        transport_kernel,
        out_shape=jax.ShapeDtypeStruct((slot_count,) + own_block.shape, own_block.dtype),
        in_specs=[pl.BlockSpec(memory_space=pl.ANY)],
        out_specs=pl.BlockSpec(memory_space=pl.ANY),
        scratch_shapes=[
            pltpu.SemaphoreType.DMA((copies, CHUNKS)),
            pltpu.SemaphoreType.DMA((slot_count, CHUNKS)),
            pltpu.SemaphoreType.DMA,
        ],
        compiler_params=pltpu.CompilerParams(collective_id=0, has_side_effects=True),
        name="transport",
    )(own_block)


def column_at(table, row_range, col_range, size, position):
    return table[(row_range * SIDE + col_range) * size + position]


def halves(block):
    high = block.astype(jnp.bfloat16)
    return high, (block - high.astype(jnp.float32)).astype(jnp.bfloat16)


def product_kernel(size, meta, table, *refs):
    lefts = refs[:STEPS]
    rights = refs[STEPS : STEPS + STEPS * GROUP]
    out_ref = refs[-1]
    row, col = meta[0], meta[1]
    for member in range(GROUP):
        position = pl.program_id(0) * GROUP + member
        target = column_at(table, row, col, size, position)
        left_parts, right_parts = [], []
        for window in range(STEPS):
            between = lax.rem(col + window, SIDE)
            reach = column_at(table, row, between, size, position) - between * size
            reached = column_at(table, between, col, size, reach)
            left_high, left_low = halves(lefts[window][0, member])
            block = rights[window * GROUP + member][0, 0]
            block = lax.cond(meta[8 + window] > 0, lambda b: b.T, lambda b: b, block)
            block = jnp.where(reached == target, block, 0.0)
            right_high, right_low = halves(block)
            left_parts += [left_high, left_low, left_high]
            right_parts += [right_high, right_high, right_low]
        out_ref[member] = jnp.dot(
            jnp.concatenate(left_parts, axis=1),
            jnp.concatenate(right_parts, axis=0),
            preferred_element_type=jnp.float32,
        )


def multiplied(held, meta, table):
    size, width = held.shape[1], held.shape[2]

    def left_spec(window):
        return pl.BlockSpec(
            (1, GROUP, width, width), lambda i, meta, table: (meta[2 + window], i, 0, 0)
        )

    def right_spec(window, member):
        def index_map(i, meta, table):
            row, col = meta[0], meta[1]
            between = lax.rem(col + window, SIDE)
            other = jnp.where(meta[8 + window] > 0, col, between)
            place = column_at(table, row, other, size, i * GROUP + member) - other * size
            return meta[5 + window], place, 0, 0

        return pl.BlockSpec((1, 1, width, width), index_map)

    specs = [left_spec(w) for w in range(STEPS)]
    specs += [right_spec(w, m) for w in range(STEPS) for m in range(GROUP)]
    return pl.pallas_call(
        functools.partial(product_kernel, size),
        out_shape=jax.ShapeDtypeStruct((size, width, width), jnp.float32),
        grid_spec=pltpu.PrefetchScalarGridSpec(
            num_scalar_prefetch=2,
            grid=(size // GROUP,),
            in_specs=specs,
            out_specs=pl.BlockSpec((GROUP, width, width), lambda i, meta, table: (i, 0, 0)),
        ),
        compiler_params=pltpu.CompilerParams(vmem_limit_bytes=32 * 1024 * 1024),
        name="multiply",
    )(meta, table, *([held] * len(specs)))


def device_meta(row, col):
    devices, slots, _, _, _, _ = plan()
    rows = []
    for r, c in devices:
        held = slots[(r, c)]
        left = [held[(r, (c + w) % SIDE)] for w in range(STEPS)]
        right, turned = [], []
        for w in range(STEPS):
            k = (c + w) % SIDE
            right.append(held[(k, c)] if (k, c) in held else held[(c, k)])
            turned.append(0 if (k, c) in held else 1)
        rows.append([r, c] + left + right + turned)
    return jnp.asarray(rows, jnp.int32)[row * SIDE + col]


def square_per_device(values, partner):
    table = lax.all_gather(partner[:, 0], ("row", "col")).reshape(-1)
    meta = device_meta(lax.axis_index("row"), lax.axis_index("col"))
    held = transported(values[:, 0])
    return multiplied(held, meta, table)[:, None]


def passed_along(value, axis, steps):
    count = lax.axis_size(axis)
    pairs = [(source, (source + steps) % count) for source in range(count)]
    return lax.ppermute(value, axis, pairs)


def spread(value, axis, root):
    mine = lax.axis_index(axis) == root
    return lax.psum(jnp.where(mine, value, jnp.zeros_like(value)), axis)


def per_device(values, partner):
    rows_tile = values.shape[0]
    col_count = lax.axis_size("col")
    range_count = col_count // lax.axis_size("row")
    range_size = rows_tile // range_count
    column = lax.axis_index("col")
    own_block = values[:, 0]
    own_cols = partner[:, 0]
    accumulated = jnp.zeros(own_block.shape, jnp.float32)
    carried_block = own_block
    carried_cols = own_cols
    for window in range(STEPS):
        if window > 0:
            carried_block, carried_cols = passed_along(
                (carried_block, carried_cols), "col", col_count - 1
            )
        target_range = (column + window) % col_count
        source_row = target_range // range_count
        part_index = target_range % range_count
        mine_block = lax.dynamic_slice_in_dim(own_block, part_index * range_size, range_size, 0)
        mine_cols = lax.dynamic_slice_in_dim(own_cols, part_index * range_size, range_size, 0)
        right_block, right_cols = (
            spread(mine_block, "row", source_row),
            spread(mine_cols, "row", source_row),
        )
        offsets = carried_cols - target_range * range_size
        gathered = jnp.take(right_block, offsets, axis=0)
        reached = jnp.take(right_cols, offsets, axis=0)
        product = jnp.einsum(
            "nxy,nyz->nxz",
            carried_block,
            gathered,
            precision=lax.Precision.HIGHEST,
            preferred_element_type=jnp.float32,
        )
        accumulated = accumulated + jnp.where((reached == own_cols)[:, None, None], product, 0.0)
    return accumulated[:, None]


def solution(mesh):
    square = mesh.shape["row"] == SIDE and mesh.shape["col"] == SIDE
    return jax.shard_map(
        square_per_device if square else per_device,
        mesh=mesh,
        in_specs=(P(("groups", "row"), "col", None, None), P(("groups", "row"), "col")),
        out_specs=P(("groups", "row"), "col", None, None),
        check_vma=False,
    )
```

```python
import functools
import jax
import jax.numpy as jnp
from jax import lax
from jax.experimental import pallas as pl
from jax.experimental.pallas import tpu as pltpu
from jax.sharding import PartitionSpec as P

STEPS = 3
MESH = pl.DeviceIdType.MESH
SIDE = 4
HALVES = 2
CHUNKS = 4
GROUP = 8
SLOT_LIMIT = 6

FLOWS = (
    (0, 0, 0, 1, 0, 1, 0, 0, 1, 0),
    (0, 0, 0, 2, 0, 1, 1, 0, 1, 1),
    (0, 1, 0, 2, 0, 2, 0, 0, 2, 0),
    (0, 1, 0, 3, 0, 3, 0, 0, 3, 0),
    (0, 1, 1, 1, 1, 1, 0, 1, 1, 0),
    (0, 1, 1, 2, 1, 1, 1, 1, 1, 1),
    (0, 1, 3, 1, 2, 1, 1, 2, 1, 1),
    (0, 2, 0, 3, 0, 3, 0, 0, 3, 0),
    (0, 2, 0, 0, 0, 0, 0, 0, 0, 0),
    (0, 2, 2, 2, 1, 2, 1, 1, 2, 1),
    (0, 2, 2, 3, 1, 2, 1, 1, 2, 1),
    (0, 3, 0, 0, 0, 2, 1, 0, 2, 1),
    (0, 3, 0, 1, 0, 1, 0, 0, 1, 0),
    (0, 3, 3, 3, 1, 3, 2, 1, 3, 2),
    (0, 3, 3, 1, 0, 1, 2, 0, 1, 2),
    (1, 0, 1, 1, 1, 1, 0, 1, 1, 0),
    (1, 0, 1, 2, 1, 1, 1, 1, 1, 1),
    (1, 0, 0, 0, 0, 0, 0, 0, 0, 0),
    (1, 0, 2, 0, 2, 0, 0, 2, 0, 0),
    (1, 1, 1, 2, 1, 2, 0, 1, 2, 0),
    (1, 1, 1, 3, 1, 2, 1, 1, 2, 1),
    (1, 2, 1, 3, 1, 3, 0, 1, 3, 0),
    (1, 2, 1, 0, 1, 0, 0, 1, 0, 0),
    (1, 2, 2, 2, 2, 2, 0, 2, 2, 0),
    (1, 2, 2, 3, 2, 3, 0, 2, 3, 0),
    (1, 2, 0, 2, 0, 2, 0, 0, 2, 0),
    (1, 3, 1, 0, 1, 2, 1, 1, 2, 1),
    (1, 3, 1, 1, 1, 1, 0, 1, 1, 0),
    (1, 3, 3, 3, 2, 3, 1, 2, 3, 1),
    (1, 3, 0, 3, 0, 2, 1, 0, 2, 1),
    (2, 0, 2, 1, 2, 1, 0, 2, 1, 0),
    (2, 0, 2, 2, 2, 1, 1, 2, 1, 1),
    (2, 0, 0, 0, 1, 0, 1, 1, 0, 1),
    (2, 0, 0, 1, 3, 0, 1, 3, 0, 1),
    (2, 1, 2, 2, 2, 2, 0, 2, 2, 0),
    (2, 1, 2, 3, 2, 3, 0, 2, 3, 0),
    (2, 1, 1, 1, 1, 0, 1, 1, 0, 1),
    (2, 1, 3, 1, 3, 1, 0, 3, 1, 0),
    (2, 2, 2, 3, 2, 3, 0, 2, 3, 0),
    (2, 2, 2, 0, 2, 3, 1, 2, 3, 1),
    (2, 3, 2, 0, 2, 0, 0, 2, 0, 0),
    (2, 3, 2, 1, 2, 1, 0, 2, 1, 0),
    (2, 3, 3, 3, 3, 3, 0, 3, 3, 0),
    (2, 3, 3, 0, 3, 2, 2, 3, 2, 2),
    (2, 3, 1, 3, 1, 3, 0, 1, 3, 0),
    (3, 0, 3, 1, 3, 1, 0, 3, 1, 0),
    (3, 0, 3, 2, 3, 1, 1, 3, 1, 1),
    (3, 0, 0, 0, 2, 0, 2, 2, 0, 2),
    (3, 0, 0, 1, 0, 1, 0, 0, 1, 0),
    (3, 0, 2, 0, 3, 2, 2, 3, 2, 2),
    (3, 1, 3, 2, 3, 2, 0, 3, 2, 0),
    (3, 1, 3, 3, 3, 3, 0, 3, 3, 0),
    (3, 1, 1, 1, 2, 1, 2, 2, 1, 2),
    (3, 1, 2, 1, 2, 1, 0, 2, 1, 0),
    (3, 2, 3, 3, 3, 3, 0, 3, 3, 0),
    (3, 2, 3, 0, 3, 3, 1, 3, 3, 1),
    (3, 2, 2, 2, 2, 2, 0, 2, 2, 0),
    (3, 2, 2, 0, 2, 3, 1, 2, 3, 1),
    (3, 3, 3, 0, 3, 0, 0, 3, 0, 0),
    (3, 3, 3, 1, 3, 1, 0, 3, 1, 0),
)


def split_flows():
    return [
        ((f[0], f[1]), (f[2], f[3]), (((f[4], f[5]), f[6]), ((f[7], f[8]), f[9]))) for f in FLOWS
    ]


def plan():
    devices = [(r, c) for r in range(SIDE) for c in range(SIDE)]
    slots = {device: {device: 0} for device in devices}
    for receiver, panel, _ in split_flows():
        slots[receiver][panel] = len(slots[receiver])
    slot_count = max(len(held) for held in slots.values())
    tags = {device: [] for device in devices}
    origins = {device: [None] * slot_count for device in devices}
    for receiver, panel, _ in split_flows():
        target = (slots[receiver][panel], receiver)
        tags[panel].append(target)
        origins[receiver][target[0]] = panel
    halves_of = []
    for half in range(HALVES):
        sends = {device: [] for device in devices}
        passed = {device: {} for device in devices}
        senders = {device: [None] * slot_count for device in devices}
        for receiver, panel, ways in split_flows():
            sender, hops = ways[half]
            target = (slots[receiver][panel], receiver)
            senders[receiver][target[0]] = sender
            if sender == panel:
                sends[sender].append(target)
            else:
                step = passed[sender].setdefault(slots[sender][panel], (hops, []))
                step[1].append(target)
        steps = {
            device: sorted((hops, slot, targets) for slot, (hops, targets) in passed[device].items())
            for device in devices
        }
        halves_of.append((sends, steps, senders))
    return devices, slots, slot_count, tags, origins, halves_of


def encoded(target):
    return -1 if target is None else (target[0] * SIDE + target[1][0]) * SIDE + target[1][1]


def picked(me, table):
    value = jnp.int32(table[0])
    for position in range(1, len(table)):
        if table[position] != table[0]:
            value = jnp.where(me == position, jnp.int32(table[position]), value)
    return value


def padded(items, count):
    return list(items) + [None] * (count - len(items))


def transport_kernel(own_ref, tag_ref, held_ref, tags_ref, send_sem, recv_sem, tag_send, tag_recv, own_sem):
    devices, _, slot_count, tags, origins, halves_of = plan()
    group, row, col = lax.axis_index("groups"), lax.axis_index("row"), lax.axis_index("col")
    me = row * SIDE + col
    half_rows = own_ref.shape[0] // HALVES
    chunk = half_rows // CHUNKS

    def table(entry):
        return picked(me, [encoded(entry(d)) for d in devices])

    def listed(items):
        count = max(len(items(d)) for d in devices)
        return [table(lambda d: padded(items(d), count)[k]) for k in range(count)]

    def places(items):
        return [
            table(lambda d: None if items(d)[slot] is None else (0, items(d)[slot]))
            for slot in range(slot_count)
        ]

    tag_codes = listed(lambda d: tags[d])
    origin_codes = places(lambda d: origins[d])
    send_codes, step_slots, step_codes, sender_codes, last = [], [], [], [], []
    for sends, steps, senders in halves_of:
        send_codes.append(listed(lambda d: sends[d]))
        sender_codes.append(places(lambda d: senders[d]))
        step_count = max(len(steps[d]) for d in devices)

        def step_at(d, k):
            return steps[d][k] if k < len(steps[d]) else (0, -1, [])

        step_slots.append(
            [picked(me, [step_at(d, k)[1] for d in devices]) for k in range(step_count)]
        )
        step_codes.append([listed(lambda d: step_at(d, k)[2]) for k in range(step_count)])
        last.append(
            [
                picked(
                    me,
                    [
                        int(senders[d][slot] is not None and slot not in [t[1] for t in steps[d]])
                        for d in devices
                    ],
                )
                for slot in range(slot_count)
            ]
        )

    def place(code):
        return (group, code // SIDE % SIDE, code % SIDE)

    barrier = pltpu.get_barrier_semaphore()
    for codes in [origin_codes] + sender_codes:
        for code in codes[1:]:
            @pl.when(code >= 0)
            def _():
                pl.semaphore_signal(barrier, inc=1, device_id=place(code), device_id_type=MESH)
    receivers = [
        len(tags[d])
        + sum(len(sends[d]) + sum(len(t[2]) for t in steps[d]) for sends, steps, _ in halves_of)
        for d in devices
    ]
    pl.semaphore_wait(barrier, picked(me, receivers))

    own_copy = pltpu.make_async_copy(own_ref, held_ref.at[0], own_sem.at[0])
    own_tag = pltpu.make_async_copy(tag_ref, tags_ref.at[0], own_sem.at[1])

    def tagged(code, index):
        slot = code // (SIDE * SIDE)
        return pltpu.make_async_remote_copy(
            src_ref=tag_ref,
            dst_ref=tags_ref.at[slot],
            send_sem=tag_send.at[index],
            recv_sem=tag_recv.at[slot],
            device_id=place(code),
            device_id_type=MESH,
        )

    def piece(half, q):
        return pl.ds(half * half_rows + q * chunk, chunk)

    def moved(source, slot, code, index, half, q):
        return pltpu.make_async_remote_copy(
            src_ref=source.at[piece(half, q)],
            dst_ref=held_ref.at[slot, piece(half, q)],
            send_sem=send_sem.at[half, index, q],
            recv_sem=recv_sem.at[half, slot, q],
            device_id=place(code),
            device_id_type=MESH,
        )

    def arrived(slot, half, q):
        moved(held_ref.at[slot], slot, me, 0, half, q).wait_recv()

    for index, code in enumerate(tag_codes):
        @pl.when(code >= 0)
        def _():
            tagged(code, index).start()
    own_tag.start()

    def start_own(q, carry):
        for half in range(HALVES):
            for index, code in enumerate(send_codes[half]):
                @pl.when(code >= 0)
                def _():
                    moved(own_ref, code // (SIDE * SIDE), code, index, half, q).start()
        return carry

    lax.fori_loop(0, CHUNKS, start_own, 0)
    own_copy.start()

    def pass_on(q, carry):
        for half in range(HALVES):
            index = len(send_codes[half])
            for slot, codes in zip(step_slots[half], step_codes[half]):
                @pl.when(slot >= 0)
                def _():
                    arrived(slot, half, q)
                for code in codes:
                    @pl.when(code >= 0)
                    def _():
                        target = code // (SIDE * SIDE)
                        moved(held_ref.at[slot], target, code, index, half, q).start()
                    index += 1
        return carry

    lax.fori_loop(0, CHUNKS, pass_on, 0)

    def finish(q, carry):
        for half in range(HALVES):
            for slot in range(1, slot_count):
                @pl.when(last[half][slot] > 0)
                def _():
                    arrived(slot, half, q)
            codes = send_codes[half] + [code for codes in step_codes[half] for code in codes]
            for index, code in enumerate(codes):
                @pl.when(code >= 0)
                def _():
                    moved(own_ref, 0, code, index, half, q).wait_send()
        return carry

    lax.fori_loop(0, CHUNKS, finish, 0)
    for slot in range(1, slot_count):
        @pl.when(origin_codes[slot] >= 0)
        def _():
            tagged(slot * SIDE * SIDE + me, 0).wait_recv()
    for index, code in enumerate(tag_codes):
        @pl.when(code >= 0)
        def _():
            tagged(code, index).wait_send()
    own_tag.wait()
    own_copy.wait()


def transported(own_block, own_tags):
    devices, _, slot_count, tags, _, halves_of = plan()
    copies = 0
    for sends, steps, _ in halves_of:
        fans = [max((len(t[2]) for t in steps[d][k : k + 1]), default=0) for d in devices for k in range(SLOT_LIMIT)]
        per_step = [max(fans[k::SLOT_LIMIT]) for k in range(SLOT_LIMIT)]
        copies = max(copies, max(len(sends[d]) for d in devices) + sum(per_step))
    return pl.pallas_call(
        transport_kernel,
        out_shape=(
            jax.ShapeDtypeStruct((slot_count,) + own_block.shape, own_block.dtype),
            jax.ShapeDtypeStruct((slot_count,) + own_tags.shape, own_tags.dtype),
        ),
        in_specs=[pl.BlockSpec(memory_space=pl.ANY)] * 2,
        out_specs=(pl.BlockSpec(memory_space=pl.ANY),) * 2,
        scratch_shapes=[
            pltpu.SemaphoreType.DMA((HALVES, copies, CHUNKS)),
            pltpu.SemaphoreType.DMA((HALVES, slot_count, CHUNKS)),
            pltpu.SemaphoreType.DMA((max(len(tags[d]) for d in devices),)),
            pltpu.SemaphoreType.DMA((slot_count,)),
            pltpu.SemaphoreType.DMA((2,)),
        ],
        compiler_params=pltpu.CompilerParams(collective_id=0, has_side_effects=True),
        name="transport",
    )(own_block, own_tags)


def halves(block):
    high = block.astype(jnp.bfloat16)
    return high, (block - high.astype(jnp.float32)).astype(jnp.bfloat16)


def product_kernel(size, meta, table, *refs):
    lefts = refs[:STEPS]
    rights = refs[STEPS : 2 * STEPS]
    out_ref = refs[-1]
    col = meta[1]
    for member in range(GROUP):
        position = pl.program_id(0) * GROUP + member
        target = table[position]
        left_parts, right_parts = [], []
        for window in range(STEPS):
            turned = meta[8 + window] > 0
            between = table[meta[2 + window] * size + position]
            reach = between - lax.rem(col + window, SIDE) * size
            place = jnp.where(turned, target - col * size, reach)
            reached = table[meta[5 + window] * size + place]
            matches = reached == jnp.where(turned, between, target)
            left_high, left_low = halves(lefts[window][0, member])
            block = rights[window][0, place]
            block = lax.cond(turned, lambda b: b.T, lambda b: b, block)
            block = jnp.where(matches, block, 0.0)
            right_high, right_low = halves(block)
            left_parts += [left_high, left_low, left_high]
            right_parts += [right_high, right_high, right_low]
        out_ref[member] = jnp.dot(
            jnp.concatenate(left_parts, axis=1),
            jnp.concatenate(right_parts, axis=0),
            preferred_element_type=jnp.float32,
        )


def multiplied(held, meta, table):
    size, width = held.shape[1], held.shape[2]

    def left_spec(window):
        return pl.BlockSpec(
            (1, GROUP, width, width), lambda i, meta, table: (meta[2 + window], i, 0, 0)
        )

    def right_spec(window):
        return pl.BlockSpec(
            (1, size, width, width),
            lambda i, meta, table: (meta[5 + window], 0, 0, 0),
            pipeline_mode=pl.Buffered(1),
        )

    specs = [left_spec(w) for w in range(STEPS)] + [right_spec(w) for w in range(STEPS)]
    return pl.pallas_call(
        functools.partial(product_kernel, size),
        out_shape=jax.ShapeDtypeStruct((size, width, width), jnp.float32),
        grid_spec=pltpu.PrefetchScalarGridSpec(
            num_scalar_prefetch=2,
            grid=(size // GROUP,),
            in_specs=specs,
            out_specs=pl.BlockSpec((GROUP, width, width), lambda i, meta, table: (i, 0, 0)),
        ),
        compiler_params=pltpu.CompilerParams(vmem_limit_bytes=48 * 1024 * 1024),
        name="multiply",
    )(meta, table, *([held] * len(specs)))


def device_meta(row, col):
    devices, slots = plan()[:2]
    rows = []
    for r, c in devices:
        held = slots[(r, c)]
        left = [held[(r, (c + w) % SIDE)] for w in range(STEPS)]
        right, turned = [], []
        for w in range(STEPS):
            k = (c + w) % SIDE
            right.append(held[(k, c)] if (k, c) in held else held[(c, k)])
            turned.append(0 if (k, c) in held else 1)
        rows.append([r, c] + left + right + turned)
    return jnp.asarray(rows, jnp.int32)[row * SIDE + col]


def square_per_device(values, partner):
    size = partner.shape[0]
    meta = device_meta(lax.axis_index("row"), lax.axis_index("col"))
    tags = jnp.broadcast_to(partner[:, 0][None, :], (8, size))
    held, held_tags = transported(values[:, 0], tags)
    return multiplied(held, meta, held_tags[:, 0, :].reshape(-1))[:, None]


def passed_along(value, axis, steps):
    count = lax.axis_size(axis)
    pairs = [(source, (source + steps) % count) for source in range(count)]
    return lax.ppermute(value, axis, pairs)


def spread(value, axis, root):
    mine = lax.axis_index(axis) == root
    return lax.psum(jnp.where(mine, value, jnp.zeros_like(value)), axis)


def per_device(values, partner):
    rows_tile = values.shape[0]
    col_count = lax.axis_size("col")
    range_count = col_count // lax.axis_size("row")
    range_size = rows_tile // range_count
    column = lax.axis_index("col")
    own_block = values[:, 0]
    own_cols = partner[:, 0]
    accumulated = jnp.zeros(own_block.shape, jnp.float32)
    carried_block = own_block
    carried_cols = own_cols
    for window in range(STEPS):
        if window > 0:
            carried_block, carried_cols = passed_along(
                (carried_block, carried_cols), "col", col_count - 1
            )
        target_range = (column + window) % col_count
        source_row = target_range // range_count
        part_index = target_range % range_count
        mine_block = lax.dynamic_slice_in_dim(own_block, part_index * range_size, range_size, 0)
        mine_cols = lax.dynamic_slice_in_dim(own_cols, part_index * range_size, range_size, 0)
        right_block, right_cols = (
            spread(mine_block, "row", source_row),
            spread(mine_cols, "row", source_row),
        )
        offsets = carried_cols - target_range * range_size
        gathered = jnp.take(right_block, offsets, axis=0)
        reached = jnp.take(right_cols, offsets, axis=0)
        product = jnp.einsum(
            "nxy,nyz->nxz",
            carried_block,
            gathered,
            precision=lax.Precision.HIGHEST,
            preferred_element_type=jnp.float32,
        )
        accumulated = accumulated + jnp.where((reached == own_cols)[:, None, None], product, 0.0)
    return accumulated[:, None]


def solution(mesh):
    square = mesh.shape["row"] == SIDE and mesh.shape["col"] == SIDE
    return jax.shard_map(
        square_per_device if square else per_device,
        mesh=mesh,
        in_specs=(P(("groups", "row"), "col", None, None), P(("groups", "row"), "col")),
        out_specs=P(("groups", "row"), "col", None, None),
        check_vma=False,
    )
```

```python
import functools
import jax
import jax.numpy as jnp
from jax import lax
from jax.experimental import pallas as pl
from jax.experimental.pallas import tpu as pltpu
from jax.sharding import PartitionSpec as P

STEPS = 3
MESH = pl.DeviceIdType.MESH
SIDE = 4
HALVES = 2
CHUNKS = 4
GROUP = 8
SLOT_LIMIT = 6

FLOWS = (
    (0, 0, 0, 1, 0, 1, 0, 0, 1, 0),
    (0, 0, 0, 2, 0, 2, 0, 0, 2, 0),
    (0, 1, 0, 2, 0, 0, 1, 0, 0, 1),
    (0, 1, 0, 3, 0, 3, 0, 0, 3, 0),
    (0, 1, 1, 1, 1, 1, 0, 1, 1, 0),
    (0, 1, 1, 2, 1, 1, 1, 1, 1, 1),
    (0, 1, 3, 1, 2, 1, 1, 2, 1, 1),
    (0, 2, 0, 3, 0, 3, 0, 0, 3, 0),
    (0, 2, 0, 0, 0, 0, 0, 0, 0, 0),
    (0, 2, 2, 2, 1, 2, 1, 1, 2, 1),
    (0, 2, 2, 3, 1, 2, 1, 1, 2, 1),
    (0, 3, 0, 0, 0, 2, 1, 0, 2, 1),
    (0, 3, 0, 1, 0, 1, 0, 0, 1, 0),
    (0, 3, 3, 3, 1, 3, 2, 1, 3, 1),
    (0, 3, 3, 1, 0, 1, 2, 0, 1, 2),
    (1, 0, 1, 1, 1, 1, 0, 1, 1, 0),
    (1, 0, 1, 2, 1, 1, 1, 1, 1, 1),
    (1, 0, 0, 0, 0, 0, 0, 0, 0, 0),
    (1, 0, 2, 0, 2, 0, 0, 2, 0, 0),
    (1, 1, 1, 2, 1, 2, 0, 1, 2, 0),
    (1, 1, 1, 3, 1, 3, 0, 1, 3, 0),
    (1, 2, 1, 3, 1, 3, 0, 1, 3, 0),
    (1, 2, 1, 0, 1, 0, 0, 1, 3, 1),
    (1, 2, 2, 2, 2, 2, 0, 2, 2, 0),
    (1, 2, 2, 3, 2, 3, 0, 2, 3, 0),
    (1, 2, 0, 2, 0, 2, 0, 0, 2, 0),
    (1, 3, 1, 0, 1, 2, 1, 1, 0, 0),
    (1, 3, 1, 1, 1, 1, 0, 1, 1, 0),
    (1, 3, 3, 3, 2, 3, 1, 3, 3, 0),
    (1, 3, 0, 3, 0, 3, 0, 0, 3, 0),
    (2, 0, 2, 1, 2, 1, 0, 2, 1, 0),
    (2, 0, 2, 2, 2, 1, 1, 2, 2, 0),
    (2, 0, 0, 0, 1, 0, 1, 1, 0, 1),
    (2, 0, 0, 1, 3, 0, 1, 3, 0, 1),
    (2, 1, 2, 2, 2, 2, 0, 2, 0, 1),
    (2, 1, 2, 3, 2, 3, 0, 2, 3, 0),
    (2, 1, 1, 1, 1, 1, 0, 1, 1, 0),
    (2, 1, 3, 1, 3, 1, 0, 3, 1, 0),
    (2, 2, 2, 3, 2, 3, 0, 2, 3, 0),
    (2, 2, 2, 0, 2, 3, 1, 2, 3, 1),
    (2, 3, 2, 0, 2, 0, 0, 2, 0, 0),
    (2, 3, 2, 1, 2, 1, 0, 2, 1, 0),
    (2, 3, 3, 3, 3, 3, 0, 3, 3, 0),
    (2, 3, 0, 3, 1, 3, 1, 1, 3, 1),
    (2, 3, 1, 3, 1, 3, 0, 1, 3, 0),
    (3, 0, 3, 1, 3, 1, 0, 3, 1, 0),
    (3, 0, 3, 2, 3, 1, 1, 3, 1, 1),
    (3, 0, 0, 0, 2, 0, 2, 2, 0, 2),
    (3, 0, 0, 1, 0, 1, 0, 0, 1, 0),
    (3, 0, 2, 0, 3, 2, 2, 3, 2, 2),
    (3, 1, 3, 2, 3, 2, 0, 3, 2, 0),
    (3, 1, 3, 3, 3, 3, 0, 3, 3, 0),
    (3, 1, 1, 1, 2, 1, 1, 2, 1, 1),
    (3, 1, 2, 1, 2, 1, 0, 3, 3, 2),
    (3, 2, 3, 3, 3, 3, 0, 3, 3, 0),
    (3, 2, 3, 0, 3, 0, 0, 3, 0, 0),
    (3, 2, 2, 2, 2, 2, 0, 2, 2, 0),
    (3, 2, 2, 0, 2, 3, 1, 2, 3, 1),
    (3, 3, 3, 0, 3, 2, 1, 3, 2, 1),
    (3, 3, 3, 1, 3, 1, 0, 3, 1, 0),
    (3, 3, 2, 1, -1, -1, 0, 2, 3, 1),
)


def split_flows():
    return [
        ((f[0], f[1]), (f[2], f[3]), (((f[4], f[5]), f[6]), ((f[7], f[8]), f[9]))) for f in FLOWS
    ]


def plan():
    devices = [(r, c) for r in range(SIDE) for c in range(SIDE)]
    slots = {device: {device: 0} for device in devices}
    for receiver, panel, _ in split_flows():
        slots[receiver][panel] = len(slots[receiver])
    slot_count = max(len(held) for held in slots.values())
    tags = {device: [] for device in devices}
    origins = {device: [None] * slot_count for device in devices}
    for receiver, panel, _ in split_flows():
        target = (slots[receiver][panel], receiver)
        tags[panel].append(target)
        origins[receiver][target[0]] = panel
    halves_of = []
    for half in range(HALVES):
        sends = {device: [] for device in devices}
        passed = {device: {} for device in devices}
        senders = {device: [None] * slot_count for device in devices}
        for receiver, panel, ways in split_flows():
            sender, hops = ways[half]
            if sender not in devices:
                continue
            target = (slots[receiver][panel], receiver)
            senders[receiver][target[0]] = sender
            if sender == panel:
                sends[sender].append(target)
            else:
                step = passed[sender].setdefault(slots[sender][panel], (hops, []))
                step[1].append(target)
        steps = {
            device: sorted((hops, slot, targets) for slot, (hops, targets) in passed[device].items())
            for device in devices
        }
        halves_of.append((sends, steps, senders))
    return devices, slots, slot_count, tags, origins, halves_of


def encoded(target):
    return -1 if target is None else (target[0] * SIDE + target[1][0]) * SIDE + target[1][1]


def picked(me, table):
    value = jnp.int32(table[0])
    for position in range(1, len(table)):
        if table[position] != table[0]:
            value = jnp.where(me == position, jnp.int32(table[position]), value)
    return value


def padded(items, count):
    return list(items) + [None] * (count - len(items))


def transport_kernel(own_ref, tag_ref, held_ref, tags_ref, send_sem, recv_sem, tag_send, tag_recv, own_sem):
    devices, _, slot_count, tags, origins, halves_of = plan()
    group, row, col = lax.axis_index("groups"), lax.axis_index("row"), lax.axis_index("col")
    me = row * SIDE + col
    half_rows = own_ref.shape[0] // HALVES
    chunk = half_rows // CHUNKS

    def table(entry):
        return picked(me, [encoded(entry(d)) for d in devices])

    def listed(items):
        count = max(len(items(d)) for d in devices)
        return [table(lambda d: padded(items(d), count)[k]) for k in range(count)]

    def places(items):
        return [
            table(lambda d: None if items(d)[slot] is None else (0, items(d)[slot]))
            for slot in range(slot_count)
        ]

    tag_codes = listed(lambda d: tags[d])
    origin_codes = places(lambda d: origins[d])
    send_codes, step_slots, step_codes, sender_codes, last = [], [], [], [], []
    for sends, steps, senders in halves_of:
        send_codes.append(listed(lambda d: sends[d]))
        sender_codes.append(places(lambda d: senders[d]))
        step_count = max(len(steps[d]) for d in devices)

        def step_at(d, k):
            return steps[d][k] if k < len(steps[d]) else (0, -1, [])

        step_slots.append(
            [picked(me, [step_at(d, k)[1] for d in devices]) for k in range(step_count)]
        )
        step_codes.append([listed(lambda d: step_at(d, k)[2]) for k in range(step_count)])
        last.append(
            [
                picked(
                    me,
                    [
                        int(senders[d][slot] is not None and slot not in [t[1] for t in steps[d]])
                        for d in devices
                    ],
                )
                for slot in range(slot_count)
            ]
        )

    def place(code):
        return (group, code // SIDE % SIDE, code % SIDE)

    barrier = pltpu.get_barrier_semaphore()
    for codes in [origin_codes] + sender_codes:
        for code in codes[1:]:
            @pl.when(code >= 0)
            def _():
                pl.semaphore_signal(barrier, inc=1, device_id=place(code), device_id_type=MESH)
    receivers = [
        len(tags[d])
        + sum(len(sends[d]) + sum(len(t[2]) for t in steps[d]) for sends, steps, _ in halves_of)
        for d in devices
    ]
    pl.semaphore_wait(barrier, picked(me, receivers))

    own_copy = pltpu.make_async_copy(own_ref, held_ref.at[0], own_sem.at[0])
    own_tag = pltpu.make_async_copy(tag_ref, tags_ref.at[0], own_sem.at[1])

    def tagged(code, index):
        slot = code // (SIDE * SIDE)
        return pltpu.make_async_remote_copy(
            src_ref=tag_ref,
            dst_ref=tags_ref.at[slot],
            send_sem=tag_send.at[index],
            recv_sem=tag_recv.at[slot],
            device_id=place(code),
            device_id_type=MESH,
        )

    def piece(half, q):
        return pl.ds(half * half_rows + q * chunk, chunk)

    def moved(source, slot, code, index, half, q):
        return pltpu.make_async_remote_copy(
            src_ref=source.at[piece(half, q)],
            dst_ref=held_ref.at[slot, piece(half, q)],
            send_sem=send_sem.at[half, index, q],
            recv_sem=recv_sem.at[half, slot, q],
            device_id=place(code),
            device_id_type=MESH,
        )

    def arrived(slot, half, q):
        moved(held_ref.at[slot], slot, me, 0, half, q).wait_recv()

    for index, code in enumerate(tag_codes):
        @pl.when(code >= 0)
        def _():
            tagged(code, index).start()
    own_tag.start()

    def start_own(q, carry):
        for half in range(HALVES):
            for index, code in enumerate(send_codes[half]):
                @pl.when(code >= 0)
                def _():
                    moved(own_ref, code // (SIDE * SIDE), code, index, half, q).start()
        return carry

    lax.fori_loop(0, CHUNKS, start_own, 0)
    own_copy.start()

    def pass_on(q, carry):
        for half in range(HALVES):
            index = len(send_codes[half])
            for slot, codes in zip(step_slots[half], step_codes[half]):
                @pl.when(slot >= 0)
                def _():
                    arrived(slot, half, q)
                for code in codes:
                    @pl.when(code >= 0)
                    def _():
                        target = code // (SIDE * SIDE)
                        moved(held_ref.at[slot], target, code, index, half, q).start()
                    index += 1
        return carry

    lax.fori_loop(0, CHUNKS, pass_on, 0)

    def finish(q, carry):
        for half in range(HALVES):
            for slot in range(1, slot_count):
                @pl.when(last[half][slot] > 0)
                def _():
                    arrived(slot, half, q)
            codes = send_codes[half] + [code for codes in step_codes[half] for code in codes]
            for index, code in enumerate(codes):
                @pl.when(code >= 0)
                def _():
                    moved(own_ref, 0, code, index, half, q).wait_send()
        return carry

    lax.fori_loop(0, CHUNKS, finish, 0)
    for slot in range(1, slot_count):
        @pl.when(origin_codes[slot] >= 0)
        def _():
            tagged(slot * SIDE * SIDE + me, 0).wait_recv()
    for index, code in enumerate(tag_codes):
        @pl.when(code >= 0)
        def _():
            tagged(code, index).wait_send()
    own_tag.wait()
    own_copy.wait()


def transported(own_block, own_tags):
    devices, _, slot_count, tags, _, halves_of = plan()
    copies = 0
    for sends, steps, _ in halves_of:
        fans = [max((len(t[2]) for t in steps[d][k : k + 1]), default=0) for d in devices for k in range(SLOT_LIMIT)]
        per_step = [max(fans[k::SLOT_LIMIT]) for k in range(SLOT_LIMIT)]
        copies = max(copies, max(len(sends[d]) for d in devices) + sum(per_step))
    return pl.pallas_call(
        transport_kernel,
        out_shape=(
            jax.ShapeDtypeStruct((slot_count,) + own_block.shape, own_block.dtype),
            jax.ShapeDtypeStruct((slot_count,) + own_tags.shape, own_tags.dtype),
        ),
        in_specs=[pl.BlockSpec(memory_space=pl.ANY)] * 2,
        out_specs=(pl.BlockSpec(memory_space=pl.ANY),) * 2,
        scratch_shapes=[
            pltpu.SemaphoreType.DMA((HALVES, copies, CHUNKS)),
            pltpu.SemaphoreType.DMA((HALVES, slot_count, CHUNKS)),
            pltpu.SemaphoreType.DMA((max(len(tags[d]) for d in devices),)),
            pltpu.SemaphoreType.DMA((slot_count,)),
            pltpu.SemaphoreType.DMA((2,)),
        ],
        compiler_params=pltpu.CompilerParams(collective_id=0, has_side_effects=True),
        name="transport",
    )(own_block, own_tags)


def halves(block):
    high = block.astype(jnp.bfloat16)
    return high, (block - high.astype(jnp.float32)).astype(jnp.bfloat16)


def product_kernel(size, meta, table, *refs):
    lefts = refs[:STEPS]
    rights = refs[STEPS : 2 * STEPS]
    out_ref = refs[-1]
    col = meta[1]
    for member in range(GROUP):
        position = pl.program_id(0) * GROUP + member
        target = table[position]
        left_parts, right_parts = [], []
        for window in range(STEPS):
            turned = meta[8 + window] > 0
            between = table[meta[2 + window] * size + position]
            reach = between - lax.rem(col + window, SIDE) * size
            place = jnp.where(turned, target - col * size, reach)
            reached = table[meta[5 + window] * size + place]
            matches = reached == jnp.where(turned, between, target)
            left_high, left_low = halves(lefts[window][0, member])
            block = rights[window][0, place]
            block = lax.cond(turned, lambda b: b.T, lambda b: b, block)
            block = jnp.where(matches, block, 0.0)
            right_high, right_low = halves(block)
            left_parts.append(jnp.concatenate([left_high, left_low], axis=0))
            right_parts.append(jnp.concatenate([right_high, right_low], axis=1))
        parts = jnp.dot(
            jnp.concatenate(left_parts, axis=1),
            jnp.concatenate(right_parts, axis=0),
            preferred_element_type=jnp.float32,
        )
        width = out_ref.shape[-1]
        small = parts[:width, width:] + parts[width:, :width] + parts[width:, width:]
        out_ref[member] = parts[:width, :width] + small


def multiplied(held, meta, table):
    size, width = held.shape[1], held.shape[2]

    def left_spec(window):
        return pl.BlockSpec(
            (1, GROUP, width, width), lambda i, meta, table: (meta[2 + window], i, 0, 0)
        )

    def right_spec(window):
        return pl.BlockSpec(
            (1, size, width, width),
            lambda i, meta, table: (meta[5 + window], 0, 0, 0),
            pipeline_mode=pl.Buffered(1),
        )

    specs = [left_spec(w) for w in range(STEPS)] + [right_spec(w) for w in range(STEPS)]
    return pl.pallas_call(
        functools.partial(product_kernel, size),
        out_shape=jax.ShapeDtypeStruct((size, width, width), jnp.float32),
        grid_spec=pltpu.PrefetchScalarGridSpec(
            num_scalar_prefetch=2,
            grid=(size // GROUP,),
            in_specs=specs,
            out_specs=pl.BlockSpec((GROUP, width, width), lambda i, meta, table: (i, 0, 0)),
        ),
        compiler_params=pltpu.CompilerParams(vmem_limit_bytes=48 * 1024 * 1024),
        name="multiply",
    )(meta, table, *([held] * len(specs)))


def device_meta(row, col):
    devices, slots = plan()[:2]
    rows = []
    for r, c in devices:
        held = slots[(r, c)]
        left = [held[(r, (c + w) % SIDE)] for w in range(STEPS)]
        right, turned = [], []
        for w in range(STEPS):
            k = (c + w) % SIDE
            right.append(held[(k, c)] if (k, c) in held else held[(c, k)])
            turned.append(0 if (k, c) in held else 1)
        rows.append([r, c] + left + right + turned)
    return jnp.asarray(rows, jnp.int32)[row * SIDE + col]


def square_per_device(values, partner):
    size = partner.shape[0]
    meta = device_meta(lax.axis_index("row"), lax.axis_index("col"))
    tags = jnp.broadcast_to(partner[:, 0][None, :], (8, size))
    held, held_tags = transported(values[:, 0], tags)
    return multiplied(held, meta, held_tags[:, 0, :].reshape(-1))[:, None]


def passed_along(value, axis, steps):
    count = lax.axis_size(axis)
    pairs = [(source, (source + steps) % count) for source in range(count)]
    return lax.ppermute(value, axis, pairs)


def spread(value, axis, root):
    mine = lax.axis_index(axis) == root
    return lax.psum(jnp.where(mine, value, jnp.zeros_like(value)), axis)


def per_device(values, partner):
    rows_tile = values.shape[0]
    col_count = lax.axis_size("col")
    range_count = col_count // lax.axis_size("row")
    range_size = rows_tile // range_count
    column = lax.axis_index("col")
    own_block = values[:, 0]
    own_cols = partner[:, 0]
    accumulated = jnp.zeros(own_block.shape, jnp.float32)
    carried_block = own_block
    carried_cols = own_cols
    for window in range(STEPS):
        if window > 0:
            carried_block, carried_cols = passed_along(
                (carried_block, carried_cols), "col", col_count - 1
            )
        target_range = (column + window) % col_count
        source_row = target_range // range_count
        part_index = target_range % range_count
        mine_block = lax.dynamic_slice_in_dim(own_block, part_index * range_size, range_size, 0)
        mine_cols = lax.dynamic_slice_in_dim(own_cols, part_index * range_size, range_size, 0)
        right_block, right_cols = (
            spread(mine_block, "row", source_row),
            spread(mine_cols, "row", source_row),
        )
        offsets = carried_cols - target_range * range_size
        gathered = jnp.take(right_block, offsets, axis=0)
        reached = jnp.take(right_cols, offsets, axis=0)
        product = jnp.einsum(
            "nxy,nyz->nxz",
            carried_block,
            gathered,
            precision=lax.Precision.HIGHEST,
            preferred_element_type=jnp.float32,
        )
        accumulated = accumulated + jnp.where((reached == own_cols)[:, None, None], product, 0.0)
    return accumulated[:, None]


def solution(mesh):
    square = mesh.shape["row"] == SIDE and mesh.shape["col"] == SIDE
    return jax.shard_map(
        square_per_device if square else per_device,
        mesh=mesh,
        in_specs=(P(("groups", "row"), "col", None, None), P(("groups", "row"), "col")),
        out_specs=P(("groups", "row"), "col", None, None),
        check_vma=False,
    )
```

```python
import functools
import jax
import jax.numpy as jnp
from jax import lax
from jax.experimental import pallas as pl
from jax.experimental.pallas import tpu as pltpu
from jax.sharding import PartitionSpec as P

STEPS = 3
MESH = pl.DeviceIdType.MESH
SIDE = 4
HALVES = 2
CHUNKS = 4
GROUP = 8
SLOT_LIMIT = 6

FLOWS = (
    (0, 0, 0, 1, 0, 1, 0, 0, 1, 0),
    (0, 0, 0, 2, 0, 1, 1, 0, 1, 1),
    (0, 1, 0, 2, 0, 2, 0, 0, 2, 0),
    (0, 1, 0, 3, 0, 3, 0, 0, 3, 0),
    (0, 1, 1, 1, 1, 1, 0, 1, 1, 0),
    (0, 1, 1, 2, 1, 1, 1, 1, 1, 1),
    (0, 1, 3, 1, 2, 1, 1, 2, 1, 1),
    (0, 2, 0, 3, 0, 3, 0, 0, 3, 0),
    (0, 2, 0, 0, 0, 0, 0, 0, 0, 0),
    (0, 2, 2, 2, 1, 2, 1, 1, 2, 1),
    (0, 2, 2, 3, 1, 2, 1, 1, 2, 1),
    (0, 3, 0, 0, 0, 2, 1, 0, 2, 1),
    (0, 3, 0, 1, 0, 1, 0, 0, 1, 0),
    (0, 3, 3, 3, 1, 3, 2, 1, 3, 2),
    (0, 3, 3, 1, 0, 1, 2, 0, 1, 2),
    (1, 0, 1, 1, 1, 1, 0, 1, 1, 0),
    (1, 0, 1, 2, 1, 1, 1, 1, 1, 1),
    (1, 0, 0, 0, 0, 0, 0, 0, 0, 0),
    (1, 0, 2, 0, 2, 0, 0, 2, 0, 0),
    (1, 1, 1, 2, 1, 2, 0, 1, 2, 0),
    (1, 1, 1, 3, 1, 2, 1, 1, 2, 1),
    (1, 2, 1, 3, 1, 3, 0, 1, 3, 0),
    (1, 2, 1, 0, 1, 0, 0, 1, 0, 0),
    (1, 2, 2, 2, 2, 2, 0, 2, 2, 0),
    (1, 2, 2, 3, 2, 3, 0, 2, 3, 0),
    (1, 2, 0, 2, 0, 2, 0, 0, 2, 0),
    (1, 3, 1, 0, 1, 2, 1, 1, 2, 1),
    (1, 3, 1, 1, 1, 1, 0, 1, 1, 0),
    (1, 3, 3, 3, 2, 3, 1, 2, 3, 1),
    (1, 3, 0, 3, 0, 2, 1, 0, 2, 1),
    (2, 0, 2, 1, 2, 1, 0, 2, 1, 0),
    (2, 0, 2, 2, 2, 1, 1, 2, 1, 1),
    (2, 0, 0, 0, 1, 0, 1, 1, 0, 1),
    (2, 0, 0, 1, 3, 0, 1, 3, 0, 1),
    (2, 1, 2, 2, 2, 2, 0, 2, 2, 0),
    (2, 1, 2, 3, 2, 3, 0, 2, 3, 0),
    (2, 1, 1, 1, 1, 0, 1, 1, 0, 1),
    (2, 1, 3, 1, 3, 1, 0, 3, 1, 0),
    (2, 2, 2, 3, 2, 3, 0, 2, 3, 0),
    (2, 2, 2, 0, 2, 3, 1, 2, 3, 1),
    (2, 3, 2, 0, 2, 0, 0, 2, 0, 0),
    (2, 3, 2, 1, 2, 1, 0, 2, 1, 0),
    (2, 3, 3, 3, 3, 3, 0, 3, 3, 0),
    (2, 3, 3, 0, 3, 2, 2, 3, 2, 2),
    (2, 3, 1, 3, 1, 3, 0, 1, 3, 0),
    (3, 0, 3, 1, 3, 1, 0, 3, 1, 0),
    (3, 0, 3, 2, 3, 1, 1, 3, 1, 1),
    (3, 0, 0, 0, 2, 0, 2, 2, 0, 2),
    (3, 0, 0, 1, 0, 1, 0, 0, 1, 0),
    (3, 0, 2, 0, 3, 2, 2, 3, 2, 2),
    (3, 1, 3, 2, 3, 2, 0, 3, 2, 0),
    (3, 1, 3, 3, 3, 3, 0, 3, 3, 0),
    (3, 1, 1, 1, 2, 1, 2, 2, 1, 2),
    (3, 1, 2, 1, 2, 1, 0, 3, 3, 2),
    (3, 2, 3, 3, 3, 3, 0, 3, 3, 0),
    (3, 2, 3, 0, 3, 3, 1, 3, 3, 1),
    (3, 2, 2, 2, 2, 2, 0, 2, 2, 0),
    (3, 2, 2, 0, 2, 3, 1, 2, 3, 1),
    (3, 3, 3, 0, 3, 0, 0, 3, 0, 0),
    (3, 3, 3, 1, 3, 1, 0, 3, 1, 0),
    (3, 3, 2, 1, -1, -1, 0, 2, 3, 1),
)


def split_flows():
    return [
        ((f[0], f[1]), (f[2], f[3]), (((f[4], f[5]), f[6]), ((f[7], f[8]), f[9]))) for f in FLOWS
    ]


def plan():
    devices = [(r, c) for r in range(SIDE) for c in range(SIDE)]
    slots = {device: {device: 0} for device in devices}
    for receiver, panel, _ in split_flows():
        slots[receiver][panel] = len(slots[receiver])
    slot_count = max(len(held) for held in slots.values())
    tags = {device: [] for device in devices}
    origins = {device: [None] * slot_count for device in devices}
    for receiver, panel, _ in split_flows():
        target = (slots[receiver][panel], receiver)
        tags[panel].append(target)
        origins[receiver][target[0]] = panel
    halves_of = []
    for half in range(HALVES):
        sends = {device: [] for device in devices}
        passed = {device: {} for device in devices}
        senders = {device: [None] * slot_count for device in devices}
        for receiver, panel, ways in split_flows():
            sender, hops = ways[half]
            if sender not in devices:
                continue
            target = (slots[receiver][panel], receiver)
            senders[receiver][target[0]] = sender
            if sender == panel:
                sends[sender].append(target)
            else:
                step = passed[sender].setdefault(slots[sender][panel], (hops, []))
                step[1].append(target)
        steps = {
            device: sorted((hops, slot, targets) for slot, (hops, targets) in passed[device].items())
            for device in devices
        }
        halves_of.append((sends, steps, senders))
    return devices, slots, slot_count, tags, origins, halves_of


def encoded(target):
    return -1 if target is None else (target[0] * SIDE + target[1][0]) * SIDE + target[1][1]


def picked(me, table):
    value = jnp.int32(table[0])
    for position in range(1, len(table)):
        if table[position] != table[0]:
            value = jnp.where(me == position, jnp.int32(table[position]), value)
    return value


def padded(items, count):
    return list(items) + [None] * (count - len(items))


def transport_kernel(own_ref, tag_ref, held_ref, tags_ref, send_sem, recv_sem, tag_send, tag_recv, own_sem):
    devices, _, slot_count, tags, origins, halves_of = plan()
    group, row, col = lax.axis_index("groups"), lax.axis_index("row"), lax.axis_index("col")
    me = row * SIDE + col
    half_rows = own_ref.shape[0] // HALVES
    chunk = half_rows // CHUNKS

    def table(entry):
        return picked(me, [encoded(entry(d)) for d in devices])

    def listed(items):
        count = max(len(items(d)) for d in devices)
        return [table(lambda d: padded(items(d), count)[k]) for k in range(count)]

    def places(items):
        return [
            table(lambda d: None if items(d)[slot] is None else (0, items(d)[slot]))
            for slot in range(slot_count)
        ]

    tag_codes = listed(lambda d: tags[d])
    origin_codes = places(lambda d: origins[d])
    send_codes, step_slots, step_codes, sender_codes, last = [], [], [], [], []
    for sends, steps, senders in halves_of:
        send_codes.append(listed(lambda d: sends[d]))
        sender_codes.append(places(lambda d: senders[d]))
        step_count = max(len(steps[d]) for d in devices)

        def step_at(d, k):
            return steps[d][k] if k < len(steps[d]) else (0, -1, [])

        step_slots.append(
            [picked(me, [step_at(d, k)[1] for d in devices]) for k in range(step_count)]
        )
        step_codes.append([listed(lambda d: step_at(d, k)[2]) for k in range(step_count)])
        last.append(
            [
                picked(
                    me,
                    [
                        int(senders[d][slot] is not None and slot not in [t[1] for t in steps[d]])
                        for d in devices
                    ],
                )
                for slot in range(slot_count)
            ]
        )

    def place(code):
        return (group, code // SIDE % SIDE, code % SIDE)

    barrier = pltpu.get_barrier_semaphore()
    for codes in [origin_codes] + sender_codes:
        for code in codes[1:]:
            @pl.when(code >= 0)
            def _():
                pl.semaphore_signal(barrier, inc=1, device_id=place(code), device_id_type=MESH)
    receivers = [
        len(tags[d])
        + sum(len(sends[d]) + sum(len(t[2]) for t in steps[d]) for sends, steps, _ in halves_of)
        for d in devices
    ]
    pl.semaphore_wait(barrier, picked(me, receivers))

    own_copy = pltpu.make_async_copy(own_ref, held_ref.at[0], own_sem.at[0])
    own_tag = pltpu.make_async_copy(tag_ref, tags_ref.at[0], own_sem.at[1])

    def tagged(code, index):
        slot = code // (SIDE * SIDE)
        return pltpu.make_async_remote_copy(
            src_ref=tag_ref,
            dst_ref=tags_ref.at[slot],
            send_sem=tag_send.at[index],
            recv_sem=tag_recv.at[slot],
            device_id=place(code),
            device_id_type=MESH,
        )

    def piece(half, q):
        return pl.ds(half * half_rows + q * chunk, chunk)

    def moved(source, slot, code, index, half, q):
        return pltpu.make_async_remote_copy(
            src_ref=source.at[piece(half, q)],
            dst_ref=held_ref.at[slot, piece(half, q)],
            send_sem=send_sem.at[half, index, q],
            recv_sem=recv_sem.at[half, slot, q],
            device_id=place(code),
            device_id_type=MESH,
        )

    def arrived(slot, half, q):
        moved(held_ref.at[slot], slot, me, 0, half, q).wait_recv()

    for index, code in enumerate(tag_codes):
        @pl.when(code >= 0)
        def _():
            tagged(code, index).start()
    own_tag.start()

    def start_own(q, carry):
        for half in range(HALVES):
            for index, code in enumerate(send_codes[half]):
                @pl.when(code >= 0)
                def _():
                    moved(own_ref, code // (SIDE * SIDE), code, index, half, q).start()
        return carry

    lax.fori_loop(0, CHUNKS, start_own, 0)
    own_copy.start()

    def pass_on(q, carry):
        for half in range(HALVES):
            index = len(send_codes[half])
            for slot, codes in zip(step_slots[half], step_codes[half]):
                @pl.when(slot >= 0)
                def _():
                    arrived(slot, half, q)
                for code in codes:
                    @pl.when(code >= 0)
                    def _():
                        target = code // (SIDE * SIDE)
                        moved(held_ref.at[slot], target, code, index, half, q).start()
                    index += 1
        return carry

    lax.fori_loop(0, CHUNKS, pass_on, 0)

    def finish(q, carry):
        for half in range(HALVES):
            for slot in range(1, slot_count):
                @pl.when(last[half][slot] > 0)
                def _():
                    arrived(slot, half, q)
            codes = send_codes[half] + [code for codes in step_codes[half] for code in codes]
            for index, code in enumerate(codes):
                @pl.when(code >= 0)
                def _():
                    moved(own_ref, 0, code, index, half, q).wait_send()
        return carry

    lax.fori_loop(0, CHUNKS, finish, 0)
    for slot in range(1, slot_count):
        @pl.when(origin_codes[slot] >= 0)
        def _():
            tagged(slot * SIDE * SIDE + me, 0).wait_recv()
    for index, code in enumerate(tag_codes):
        @pl.when(code >= 0)
        def _():
            tagged(code, index).wait_send()
    own_tag.wait()
    own_copy.wait()


def transported(own_block, own_tags):
    devices, _, slot_count, tags, _, halves_of = plan()
    copies = 0
    for sends, steps, _ in halves_of:
        fans = [max((len(t[2]) for t in steps[d][k : k + 1]), default=0) for d in devices for k in range(SLOT_LIMIT)]
        per_step = [max(fans[k::SLOT_LIMIT]) for k in range(SLOT_LIMIT)]
        copies = max(copies, max(len(sends[d]) for d in devices) + sum(per_step))
    return pl.pallas_call(
        transport_kernel,
        out_shape=(
            jax.ShapeDtypeStruct((slot_count,) + own_block.shape, own_block.dtype),
            jax.ShapeDtypeStruct((slot_count,) + own_tags.shape, own_tags.dtype),
        ),
        in_specs=[pl.BlockSpec(memory_space=pl.ANY)] * 2,
        out_specs=(pl.BlockSpec(memory_space=pl.ANY),) * 2,
        scratch_shapes=[
            pltpu.SemaphoreType.DMA((HALVES, copies, CHUNKS)),
            pltpu.SemaphoreType.DMA((HALVES, slot_count, CHUNKS)),
            pltpu.SemaphoreType.DMA((max(len(tags[d]) for d in devices),)),
            pltpu.SemaphoreType.DMA((slot_count,)),
            pltpu.SemaphoreType.DMA((2,)),
        ],
        compiler_params=pltpu.CompilerParams(collective_id=0, has_side_effects=True),
        name="transport",
    )(own_block, own_tags)


def halves(block):
    high = block.astype(jnp.bfloat16)
    return high, (block - high.astype(jnp.float32)).astype(jnp.bfloat16)


def product_kernel(size, meta, table, *refs):
    lefts = refs[:STEPS]
    rights = refs[STEPS : 2 * STEPS]
    out_ref = refs[-1]
    col = meta[1]

    def members(turned):
        for member in range(GROUP):
            position = pl.program_id(0) * GROUP + member
            target = table[position]
            left_parts, right_parts = [], []
            for window in range(STEPS):
                between = table[meta[2 + window] * size + position]
                if turned[window]:
                    place, wanted = target - col * size, between
                else:
                    place, wanted = between - lax.rem(col + window, SIDE) * size, target
                matches = table[meta[5 + window] * size + place] == wanted
                left_high, left_low = halves(lefts[window][0, member])
                block = rights[window][0, place]
                block = block.T if turned[window] else block
                right_high, right_low = halves(jnp.where(matches, block, 0.0))
                left_parts += [left_high, left_low, left_high]
                right_parts += [right_high, right_high, right_low]
            out_ref[member] = jnp.dot(
                jnp.concatenate(left_parts, axis=1),
                jnp.concatenate(right_parts, axis=0),
                preferred_element_type=jnp.float32,
            )

    for second in (False, True):
        for third in (False, True):
            @pl.when(jnp.logical_and(meta[9] == int(second), meta[10] == int(third)))
            def _():
                members((False, second, third))


def multiplied(held, meta, table):
    size, width = held.shape[1], held.shape[2]

    def left_spec(window):
        return pl.BlockSpec(
            (1, GROUP, width, width), lambda i, meta, table: (meta[2 + window], i, 0, 0)
        )

    def right_spec(window):
        return pl.BlockSpec(
            (1, size, width, width),
            lambda i, meta, table: (meta[5 + window], 0, 0, 0),
            pipeline_mode=pl.Buffered(1),
        )

    specs = [left_spec(w) for w in range(STEPS)] + [right_spec(w) for w in range(STEPS)]
    return pl.pallas_call(
        functools.partial(product_kernel, size),
        out_shape=jax.ShapeDtypeStruct((size, width, width), jnp.float32),
        grid_spec=pltpu.PrefetchScalarGridSpec(
            num_scalar_prefetch=2,
            grid=(size // GROUP,),
            in_specs=specs,
            out_specs=pl.BlockSpec((GROUP, width, width), lambda i, meta, table: (i, 0, 0)),
        ),
        compiler_params=pltpu.CompilerParams(vmem_limit_bytes=48 * 1024 * 1024),
        name="multiply",
    )(meta, table, *([held] * len(specs)))


def device_meta(row, col):
    devices, slots = plan()[:2]
    rows = []
    for r, c in devices:
        held = slots[(r, c)]
        left = [held[(r, (c + w) % SIDE)] for w in range(STEPS)]
        right, turned = [], []
        for w in range(STEPS):
            k = (c + w) % SIDE
            right.append(held[(k, c)] if (k, c) in held else held[(c, k)])
            turned.append(0 if (k, c) in held else 1)
        rows.append([r, c] + left + right + turned)
    return jnp.asarray(rows, jnp.int32)[row * SIDE + col]


def square_per_device(values, partner):
    size = partner.shape[0]
    meta = device_meta(lax.axis_index("row"), lax.axis_index("col"))
    tags = jnp.broadcast_to(partner[:, 0][None, :], (8, size))
    held, held_tags = transported(values[:, 0], tags)
    return multiplied(held, meta, held_tags[:, 0, :].reshape(-1))[:, None]


def passed_along(value, axis, steps):
    count = lax.axis_size(axis)
    pairs = [(source, (source + steps) % count) for source in range(count)]
    return lax.ppermute(value, axis, pairs)


def spread(value, axis, root):
    mine = lax.axis_index(axis) == root
    return lax.psum(jnp.where(mine, value, jnp.zeros_like(value)), axis)


def per_device(values, partner):
    rows_tile = values.shape[0]
    col_count = lax.axis_size("col")
    range_count = col_count // lax.axis_size("row")
    range_size = rows_tile // range_count
    column = lax.axis_index("col")
    own_block = values[:, 0]
    own_cols = partner[:, 0]
    accumulated = jnp.zeros(own_block.shape, jnp.float32)
    carried_block = own_block
    carried_cols = own_cols
    for window in range(STEPS):
        if window > 0:
            carried_block, carried_cols = passed_along(
                (carried_block, carried_cols), "col", col_count - 1
            )
        target_range = (column + window) % col_count
        source_row = target_range // range_count
        part_index = target_range % range_count
        mine_block = lax.dynamic_slice_in_dim(own_block, part_index * range_size, range_size, 0)
        mine_cols = lax.dynamic_slice_in_dim(own_cols, part_index * range_size, range_size, 0)
        right_block, right_cols = (
            spread(mine_block, "row", source_row),
            spread(mine_cols, "row", source_row),
        )
        offsets = carried_cols - target_range * range_size
        gathered = jnp.take(right_block, offsets, axis=0)
        reached = jnp.take(right_cols, offsets, axis=0)
        product = jnp.einsum(
            "nxy,nyz->nxz",
            carried_block,
            gathered,
            precision=lax.Precision.HIGHEST,
            preferred_element_type=jnp.float32,
        )
        accumulated = accumulated + jnp.where((reached == own_cols)[:, None, None], product, 0.0)
    return accumulated[:, None]


def solution(mesh):
    square = mesh.shape["row"] == SIDE and mesh.shape["col"] == SIDE
    return jax.shard_map(
        square_per_device if square else per_device,
        mesh=mesh,
        in_specs=(P(("groups", "row"), "col", None, None), P(("groups", "row"), "col")),
        out_specs=P(("groups", "row"), "col", None, None),
        check_vma=False,
    )
```

```python
import functools
import jax
import jax.numpy as jnp
from jax import lax
from jax.experimental import pallas as pl
from jax.experimental.pallas import tpu as pltpu
from jax.sharding import PartitionSpec as P

STEPS = 3
MESH = pl.DeviceIdType.MESH
SIDE = 4
HALVES = 2
CHUNKS = 8
GROUP = 8
SLOT_LIMIT = 6

FLOWS = (
    (0, 0, 0, 1, 0, 1, 0, 0, 1, 0),
    (0, 0, 0, 2, 0, 1, 1, 0, 1, 1),
    (0, 1, 0, 2, 0, 2, 0, 0, 2, 0),
    (0, 1, 0, 3, 0, 3, 0, 0, 3, 0),
    (0, 1, 1, 1, 1, 1, 0, 1, 1, 0),
    (0, 1, 1, 2, 1, 1, 1, 1, 1, 1),
    (0, 1, 3, 1, 2, 1, 1, 2, 1, 1),
    (0, 2, 0, 3, 0, 3, 0, 0, 3, 0),
    (0, 2, 0, 0, 0, 0, 0, 0, 0, 0),
    (0, 2, 2, 2, 1, 2, 1, 1, 2, 1),
    (0, 2, 2, 3, 1, 2, 1, 1, 2, 1),
    (0, 3, 0, 0, 0, 2, 1, 0, 2, 1),
    (0, 3, 0, 1, 0, 1, 0, 0, 1, 0),
    (0, 3, 3, 3, 1, 3, 2, 1, 3, 2),
    (0, 3, 3, 1, 0, 1, 2, 0, 1, 2),
    (1, 0, 1, 1, 1, 1, 0, 1, 1, 0),
    (1, 0, 1, 2, 1, 1, 1, 1, 1, 1),
    (1, 0, 0, 0, 0, 0, 0, 0, 0, 0),
    (1, 0, 2, 0, 2, 0, 0, 2, 0, 0),
    (1, 1, 1, 2, 1, 2, 0, 1, 2, 0),
    (1, 1, 1, 3, 1, 2, 1, 1, 2, 1),
    (1, 2, 1, 3, 1, 3, 0, 1, 3, 0),
    (1, 2, 1, 0, 1, 0, 0, 1, 0, 0),
    (1, 2, 2, 2, 2, 2, 0, 2, 2, 0),
    (1, 2, 2, 3, 2, 3, 0, 2, 3, 0),
    (1, 2, 0, 2, 0, 2, 0, 0, 2, 0),
    (1, 3, 1, 0, 1, 2, 1, 1, 2, 1),
    (1, 3, 1, 1, 1, 1, 0, 1, 1, 0),
    (1, 3, 3, 3, 2, 3, 1, 2, 3, 1),
    (1, 3, 0, 3, 0, 2, 1, 0, 2, 1),
    (2, 0, 2, 1, 2, 1, 0, 2, 1, 0),
    (2, 0, 2, 2, 2, 1, 1, 2, 1, 1),
    (2, 0, 0, 0, 1, 0, 1, 1, 0, 1),
    (2, 0, 0, 1, 3, 0, 1, 3, 0, 1),
    (2, 1, 2, 2, 2, 2, 0, 2, 2, 0),
    (2, 1, 2, 3, 2, 3, 0, 2, 3, 0),
    (2, 1, 1, 1, 1, 0, 1, 1, 0, 1),
    (2, 1, 3, 1, 3, 1, 0, 3, 1, 0),
    (2, 2, 2, 3, 2, 3, 0, 2, 3, 0),
    (2, 2, 2, 0, 2, 3, 1, 2, 3, 1),
    (2, 3, 2, 0, 2, 0, 0, 2, 0, 0),
    (2, 3, 2, 1, 2, 1, 0, 2, 1, 0),
    (2, 3, 3, 3, 3, 3, 0, 3, 3, 0),
    (2, 3, 3, 0, 3, 2, 2, 3, 2, 2),
    (2, 3, 1, 3, 1, 3, 0, 1, 3, 0),
    (3, 0, 3, 1, 3, 1, 0, 3, 1, 0),
    (3, 0, 3, 2, 3, 1, 1, 3, 1, 1),
    (3, 0, 0, 0, 2, 0, 2, 2, 0, 2),
    (3, 0, 0, 1, 0, 1, 0, 0, 1, 0),
    (3, 0, 2, 0, 3, 2, 2, 3, 2, 2),
    (3, 1, 3, 2, 3, 2, 0, 3, 2, 0),
    (3, 1, 3, 3, 3, 3, 0, 3, 3, 0),
    (3, 1, 1, 1, 2, 1, 2, 2, 1, 2),
    (3, 1, 2, 1, 2, 1, 0, 3, 3, 2),
    (3, 2, 3, 3, 3, 3, 0, 3, 3, 0),
    (3, 2, 3, 0, 3, 3, 1, 3, 3, 1),
    (3, 2, 2, 2, 2, 2, 0, 2, 2, 0),
    (3, 2, 2, 0, 2, 3, 1, 2, 3, 1),
    (3, 3, 3, 0, 3, 0, 0, 3, 0, 0),
    (3, 3, 3, 1, 3, 1, 0, 3, 1, 0),
    (3, 3, 2, 1, -1, -1, 0, 2, 3, 1),
)


def split_flows():
    return [
        ((f[0], f[1]), (f[2], f[3]), (((f[4], f[5]), f[6]), ((f[7], f[8]), f[9]))) for f in FLOWS
    ]


def plan():
    devices = [(r, c) for r in range(SIDE) for c in range(SIDE)]
    slots = {device: {device: 0} for device in devices}
    for receiver, panel, _ in split_flows():
        slots[receiver][panel] = len(slots[receiver])
    slot_count = max(len(held) for held in slots.values())
    tags = {device: [] for device in devices}
    origins = {device: [None] * slot_count for device in devices}
    for receiver, panel, _ in split_flows():
        target = (slots[receiver][panel], receiver)
        tags[panel].append(target)
        origins[receiver][target[0]] = panel
    halves_of = []
    for half in range(HALVES):
        sends = {device: [] for device in devices}
        passed = {device: {} for device in devices}
        senders = {device: [None] * slot_count for device in devices}
        for receiver, panel, ways in split_flows():
            sender, hops = ways[half]
            if sender not in devices:
                continue
            target = (slots[receiver][panel], receiver)
            senders[receiver][target[0]] = sender
            if sender == panel:
                sends[sender].append(target)
            else:
                step = passed[sender].setdefault(slots[sender][panel], (hops, []))
                step[1].append(target)
        steps = {
            device: sorted((hops, slot, targets) for slot, (hops, targets) in passed[device].items())
            for device in devices
        }
        halves_of.append((sends, steps, senders))
    return devices, slots, slot_count, tags, origins, halves_of


def encoded(target):
    return -1 if target is None else (target[0] * SIDE + target[1][0]) * SIDE + target[1][1]


def picked(me, table):
    value = jnp.int32(table[0])
    for position in range(1, len(table)):
        if table[position] != table[0]:
            value = jnp.where(me == position, jnp.int32(table[position]), value)
    return value


def padded(items, count):
    return list(items) + [None] * (count - len(items))


def transport_kernel(own_ref, tag_ref, held_ref, tags_ref, send_sem, recv_sem, tag_send, tag_recv, own_sem):
    devices, _, slot_count, tags, origins, halves_of = plan()
    group, row, col = lax.axis_index("groups"), lax.axis_index("row"), lax.axis_index("col")
    me = row * SIDE + col
    half_rows = own_ref.shape[0] // HALVES
    chunk = half_rows // CHUNKS

    def table(entry):
        return picked(me, [encoded(entry(d)) for d in devices])

    def listed(items):
        count = max(len(items(d)) for d in devices)
        return [table(lambda d: padded(items(d), count)[k]) for k in range(count)]

    def places(items):
        return [
            table(lambda d: None if items(d)[slot] is None else (0, items(d)[slot]))
            for slot in range(slot_count)
        ]

    tag_codes = listed(lambda d: tags[d])
    origin_codes = places(lambda d: origins[d])
    send_codes, step_slots, step_codes, sender_codes, last = [], [], [], [], []
    for sends, steps, senders in halves_of:
        send_codes.append(listed(lambda d: sends[d]))
        sender_codes.append(places(lambda d: senders[d]))
        step_count = max(len(steps[d]) for d in devices)

        def step_at(d, k):
            return steps[d][k] if k < len(steps[d]) else (0, -1, [])

        step_slots.append(
            [picked(me, [step_at(d, k)[1] for d in devices]) for k in range(step_count)]
        )
        step_codes.append([listed(lambda d: step_at(d, k)[2]) for k in range(step_count)])
        last.append(
            [
                picked(
                    me,
                    [
                        int(senders[d][slot] is not None and slot not in [t[1] for t in steps[d]])
                        for d in devices
                    ],
                )
                for slot in range(slot_count)
            ]
        )

    def place(code):
        return (group, code // SIDE % SIDE, code % SIDE)

    barrier = pltpu.get_barrier_semaphore()
    for codes in [origin_codes] + sender_codes:
        for code in codes[1:]:
            @pl.when(code >= 0)
            def _():
                pl.semaphore_signal(barrier, inc=1, device_id=place(code), device_id_type=MESH)
    receivers = [
        len(tags[d])
        + sum(len(sends[d]) + sum(len(t[2]) for t in steps[d]) for sends, steps, _ in halves_of)
        for d in devices
    ]
    pl.semaphore_wait(barrier, picked(me, receivers))

    own_copy = pltpu.make_async_copy(own_ref, held_ref.at[0], own_sem.at[0])
    own_tag = pltpu.make_async_copy(tag_ref, tags_ref.at[0], own_sem.at[1])

    def tagged(code, index):
        slot = code // (SIDE * SIDE)
        return pltpu.make_async_remote_copy(
            src_ref=tag_ref,
            dst_ref=tags_ref.at[slot],
            send_sem=tag_send.at[index],
            recv_sem=tag_recv.at[slot],
            device_id=place(code),
            device_id_type=MESH,
        )

    def piece(half, q):
        return pl.ds(half * half_rows + q * chunk, chunk)

    def moved(source, slot, code, index, half, q):
        return pltpu.make_async_remote_copy(
            src_ref=source.at[piece(half, q)],
            dst_ref=held_ref.at[slot, piece(half, q)],
            send_sem=send_sem.at[half, index, q],
            recv_sem=recv_sem.at[half, slot, q],
            device_id=place(code),
            device_id_type=MESH,
        )

    def arrived(slot, half, q):
        moved(held_ref.at[slot], slot, me, 0, half, q).wait_recv()

    for index, code in enumerate(tag_codes):
        @pl.when(code >= 0)
        def _():
            tagged(code, index).start()
    own_tag.start()

    def start_own(q, carry):
        for half in range(HALVES):
            for index, code in enumerate(send_codes[half]):
                @pl.when(code >= 0)
                def _():
                    moved(own_ref, code // (SIDE * SIDE), code, index, half, q).start()
        return carry

    lax.fori_loop(0, CHUNKS, start_own, 0)
    own_copy.start()

    def pass_on(q, carry):
        for half in range(HALVES):
            index = len(send_codes[half])
            for slot, codes in zip(step_slots[half], step_codes[half]):
                @pl.when(slot >= 0)
                def _():
                    arrived(slot, half, q)
                for code in codes:
                    @pl.when(code >= 0)
                    def _():
                        target = code // (SIDE * SIDE)
                        moved(held_ref.at[slot], target, code, index, half, q).start()
                    index += 1
        return carry

    lax.fori_loop(0, CHUNKS, pass_on, 0)

    def finish(q, carry):
        for half in range(HALVES):
            for slot in range(1, slot_count):
                @pl.when(last[half][slot] > 0)
                def _():
                    arrived(slot, half, q)
            codes = send_codes[half] + [code for codes in step_codes[half] for code in codes]
            for index, code in enumerate(codes):
                @pl.when(code >= 0)
                def _():
                    moved(own_ref, 0, code, index, half, q).wait_send()
        return carry

    lax.fori_loop(0, CHUNKS, finish, 0)
    for slot in range(1, slot_count):
        @pl.when(origin_codes[slot] >= 0)
        def _():
            tagged(slot * SIDE * SIDE + me, 0).wait_recv()
    for index, code in enumerate(tag_codes):
        @pl.when(code >= 0)
        def _():
            tagged(code, index).wait_send()
    own_tag.wait()
    own_copy.wait()


def transported(own_block, own_tags):
    devices, _, slot_count, tags, _, halves_of = plan()
    copies = 0
    for sends, steps, _ in halves_of:
        fans = [max((len(t[2]) for t in steps[d][k : k + 1]), default=0) for d in devices for k in range(SLOT_LIMIT)]
        per_step = [max(fans[k::SLOT_LIMIT]) for k in range(SLOT_LIMIT)]
        copies = max(copies, max(len(sends[d]) for d in devices) + sum(per_step))
    return pl.pallas_call(
        transport_kernel,
        out_shape=(
            jax.ShapeDtypeStruct((slot_count,) + own_block.shape, own_block.dtype),
            jax.ShapeDtypeStruct((slot_count,) + own_tags.shape, own_tags.dtype),
        ),
        in_specs=[pl.BlockSpec(memory_space=pl.ANY)] * 2,
        out_specs=(pl.BlockSpec(memory_space=pl.ANY),) * 2,
        scratch_shapes=[
            pltpu.SemaphoreType.DMA((HALVES, copies, CHUNKS)),
            pltpu.SemaphoreType.DMA((HALVES, slot_count, CHUNKS)),
            pltpu.SemaphoreType.DMA((max(len(tags[d]) for d in devices),)),
            pltpu.SemaphoreType.DMA((slot_count,)),
            pltpu.SemaphoreType.DMA((2,)),
        ],
        compiler_params=pltpu.CompilerParams(collective_id=0, has_side_effects=True),
        name="transport",
    )(own_block, own_tags)


def halves(block):
    high = block.astype(jnp.bfloat16)
    return high, (block - high.astype(jnp.float32)).astype(jnp.bfloat16)


def product_kernel(size, meta, table, *refs):
    lefts = refs[:STEPS]
    rights = refs[STEPS : 2 * STEPS]
    out_ref = refs[-1]
    col = meta[1]

    def members(turned):
        for member in range(GROUP):
            position = pl.program_id(0) * GROUP + member
            target = table[position]
            left_parts, right_parts = [], []
            for window in range(STEPS):
                between = table[meta[2 + window] * size + position]
                if turned[window]:
                    place, wanted = target - col * size, between
                else:
                    place, wanted = between - lax.rem(col + window, SIDE) * size, target
                matches = table[meta[5 + window] * size + place] == wanted
                left_high, left_low = halves(lefts[window][0, member])
                block = rights[window][0, place]
                block = block.T if turned[window] else block
                right_high, right_low = halves(jnp.where(matches, block, 0.0))
                left_parts += [left_high, left_low, left_high]
                right_parts += [right_high, right_high, right_low]
            out_ref[member] = jnp.dot(
                jnp.concatenate(left_parts, axis=1),
                jnp.concatenate(right_parts, axis=0),
                preferred_element_type=jnp.float32,
            )

    for second in (False, True):
        for third in (False, True):
            @pl.when(jnp.logical_and(meta[9] == int(second), meta[10] == int(third)))
            def _():
                members((False, second, third))


def multiplied(held, meta, table):
    size, width = held.shape[1], held.shape[2]

    def left_spec(window):
        return pl.BlockSpec(
            (1, GROUP, width, width), lambda i, meta, table: (meta[2 + window], i, 0, 0)
        )

    def right_spec(window):
        return pl.BlockSpec(
            (1, size, width, width),
            lambda i, meta, table: (meta[5 + window], 0, 0, 0),
            pipeline_mode=pl.Buffered(1),
        )

    specs = [left_spec(w) for w in range(STEPS)] + [right_spec(w) for w in range(STEPS)]
    return pl.pallas_call(
        functools.partial(product_kernel, size),
        out_shape=jax.ShapeDtypeStruct((size, width, width), jnp.float32),
        grid_spec=pltpu.PrefetchScalarGridSpec(
            num_scalar_prefetch=2,
            grid=(size // GROUP,),
            in_specs=specs,
            out_specs=pl.BlockSpec((GROUP, width, width), lambda i, meta, table: (i, 0, 0)),
        ),
        compiler_params=pltpu.CompilerParams(vmem_limit_bytes=48 * 1024 * 1024),
        name="multiply",
    )(meta, table, *([held] * len(specs)))


def device_meta(row, col):
    devices, slots = plan()[:2]
    rows = []
    for r, c in devices:
        held = slots[(r, c)]
        left = [held[(r, (c + w) % SIDE)] for w in range(STEPS)]
        right, turned = [], []
        for w in range(STEPS):
            k = (c + w) % SIDE
            right.append(held[(k, c)] if (k, c) in held else held[(c, k)])
            turned.append(0 if (k, c) in held else 1)
        rows.append([r, c] + left + right + turned)
    return jnp.asarray(rows, jnp.int32)[row * SIDE + col]


def square_per_device(values, partner):
    size = partner.shape[0]
    meta = device_meta(lax.axis_index("row"), lax.axis_index("col"))
    tags = jnp.broadcast_to(partner[:, 0][None, :], (8, size))
    held, held_tags = transported(values[:, 0], tags)
    return multiplied(held, meta, held_tags[:, 0, :].reshape(-1))[:, None]


def passed_along(value, axis, steps):
    count = lax.axis_size(axis)
    pairs = [(source, (source + steps) % count) for source in range(count)]
    return lax.ppermute(value, axis, pairs)


def spread(value, axis, root):
    mine = lax.axis_index(axis) == root
    return lax.psum(jnp.where(mine, value, jnp.zeros_like(value)), axis)


def per_device(values, partner):
    rows_tile = values.shape[0]
    col_count = lax.axis_size("col")
    range_count = col_count // lax.axis_size("row")
    range_size = rows_tile // range_count
    column = lax.axis_index("col")
    own_block = values[:, 0]
    own_cols = partner[:, 0]
    accumulated = jnp.zeros(own_block.shape, jnp.float32)
    carried_block = own_block
    carried_cols = own_cols
    for window in range(STEPS):
        if window > 0:
            carried_block, carried_cols = passed_along(
                (carried_block, carried_cols), "col", col_count - 1
            )
        target_range = (column + window) % col_count
        source_row = target_range // range_count
        part_index = target_range % range_count
        mine_block = lax.dynamic_slice_in_dim(own_block, part_index * range_size, range_size, 0)
        mine_cols = lax.dynamic_slice_in_dim(own_cols, part_index * range_size, range_size, 0)
        right_block, right_cols = (
            spread(mine_block, "row", source_row),
            spread(mine_cols, "row", source_row),
        )
        offsets = carried_cols - target_range * range_size
        gathered = jnp.take(right_block, offsets, axis=0)
        reached = jnp.take(right_cols, offsets, axis=0)
        product = jnp.einsum(
            "nxy,nyz->nxz",
            carried_block,
            gathered,
            precision=lax.Precision.HIGHEST,
            preferred_element_type=jnp.float32,
        )
        accumulated = accumulated + jnp.where((reached == own_cols)[:, None, None], product, 0.0)
    return accumulated[:, None]


def solution(mesh):
    square = mesh.shape["row"] == SIDE and mesh.shape["col"] == SIDE
    return jax.shard_map(
        square_per_device if square else per_device,
        mesh=mesh,
        in_specs=(P(("groups", "row"), "col", None, None), P(("groups", "row"), "col")),
        out_specs=P(("groups", "row"), "col", None, None),
        check_vma=False,
    )
```

```python
import functools
import jax
import jax.numpy as jnp
from jax import lax
from jax.experimental import pallas as pl
from jax.experimental.pallas import tpu as pltpu
from jax.sharding import PartitionSpec as P

STEPS = 3
MESH = pl.DeviceIdType.MESH
SIDE = 4
HALVES = 2
CHUNKS = 4
GROUP = 16
SLOT_LIMIT = 6

FLOWS = (
    (0, 0, 0, 1, 0, 1, 0, 0, 1, 0),
    (0, 0, 0, 2, 0, 1, 1, 0, 1, 1),
    (0, 1, 0, 2, 0, 2, 0, 0, 2, 0),
    (0, 1, 0, 3, 0, 3, 0, 0, 3, 0),
    (0, 1, 1, 1, 1, 1, 0, 1, 1, 0),
    (0, 1, 1, 2, 1, 1, 1, 1, 1, 1),
    (0, 1, 3, 1, 2, 1, 1, 2, 1, 1),
    (0, 2, 0, 3, 0, 3, 0, 0, 3, 0),
    (0, 2, 0, 0, 0, 0, 0, 0, 0, 0),
    (0, 2, 2, 2, 1, 2, 1, 1, 2, 1),
    (0, 2, 2, 3, 1, 2, 1, 1, 2, 1),
    (0, 3, 0, 0, 0, 2, 1, 0, 2, 1),
    (0, 3, 0, 1, 0, 1, 0, 0, 1, 0),
    (0, 3, 3, 3, 1, 3, 2, 1, 3, 2),
    (0, 3, 3, 1, 0, 1, 2, 0, 1, 2),
    (1, 0, 1, 1, 1, 1, 0, 1, 1, 0),
    (1, 0, 1, 2, 1, 1, 1, 1, 1, 1),
    (1, 0, 0, 0, 0, 0, 0, 0, 0, 0),
    (1, 0, 2, 0, 2, 0, 0, 2, 0, 0),
    (1, 1, 1, 2, 1, 2, 0, 1, 2, 0),
    (1, 1, 1, 3, 1, 2, 1, 1, 2, 1),
    (1, 2, 1, 3, 1, 3, 0, 1, 3, 0),
    (1, 2, 1, 0, 1, 0, 0, 1, 0, 0),
    (1, 2, 2, 2, 2, 2, 0, 2, 2, 0),
    (1, 2, 2, 3, 2, 3, 0, 2, 3, 0),
    (1, 2, 0, 2, 0, 2, 0, 0, 2, 0),
    (1, 3, 1, 0, 1, 2, 1, 1, 2, 1),
    (1, 3, 1, 1, 1, 1, 0, 1, 1, 0),
    (1, 3, 3, 3, 2, 3, 1, 2, 3, 1),
    (1, 3, 0, 3, 0, 2, 1, 0, 2, 1),
    (2, 0, 2, 1, 2, 1, 0, 2, 1, 0),
    (2, 0, 2, 2, 2, 1, 1, 2, 1, 1),
    (2, 0, 0, 0, 1, 0, 1, 1, 0, 1),
    (2, 0, 0, 1, 3, 0, 1, 3, 0, 1),
    (2, 1, 2, 2, 2, 2, 0, 2, 2, 0),
    (2, 1, 2, 3, 2, 3, 0, 2, 3, 0),
    (2, 1, 1, 1, 1, 0, 1, 1, 0, 1),
    (2, 1, 3, 1, 3, 1, 0, 3, 1, 0),
    (2, 2, 2, 3, 2, 3, 0, 2, 3, 0),
    (2, 2, 2, 0, 2, 3, 1, 2, 3, 1),
    (2, 3, 2, 0, 2, 0, 0, 2, 0, 0),
    (2, 3, 2, 1, 2, 1, 0, 2, 1, 0),
    (2, 3, 3, 3, 3, 3, 0, 3, 3, 0),
    (2, 3, 3, 0, 3, 2, 2, 3, 2, 2),
    (2, 3, 1, 3, 1, 3, 0, 1, 3, 0),
    (3, 0, 3, 1, 3, 1, 0, 3, 1, 0),
    (3, 0, 3, 2, 3, 1, 1, 3, 1, 1),
    (3, 0, 0, 0, 2, 0, 2, 2, 0, 2),
    (3, 0, 0, 1, 0, 1, 0, 0, 1, 0),
    (3, 0, 2, 0, 3, 2, 2, 3, 2, 2),
    (3, 1, 3, 2, 3, 2, 0, 3, 2, 0),
    (3, 1, 3, 3, 3, 3, 0, 3, 3, 0),
    (3, 1, 1, 1, 2, 1, 2, 2, 1, 2),
    (3, 1, 2, 1, 2, 1, 0, 3, 3, 2),
    (3, 2, 3, 3, 3, 3, 0, 3, 3, 0),
    (3, 2, 3, 0, 3, 3, 1, 3, 3, 1),
    (3, 2, 2, 2, 2, 2, 0, 2, 2, 0),
    (3, 2, 2, 0, 2, 3, 1, 2, 3, 1),
    (3, 3, 3, 0, 3, 0, 0, 3, 0, 0),
    (3, 3, 3, 1, 3, 1, 0, 3, 1, 0),
    (3, 3, 2, 1, -1, -1, 0, 2, 3, 1),
)


def split_flows():
    return [
        ((f[0], f[1]), (f[2], f[3]), (((f[4], f[5]), f[6]), ((f[7], f[8]), f[9]))) for f in FLOWS
    ]


def plan():
    devices = [(r, c) for r in range(SIDE) for c in range(SIDE)]
    slots = {device: {device: 0} for device in devices}
    for receiver, panel, _ in split_flows():
        slots[receiver][panel] = len(slots[receiver])
    slot_count = max(len(held) for held in slots.values())
    tags = {device: [] for device in devices}
    origins = {device: [None] * slot_count for device in devices}
    for receiver, panel, _ in split_flows():
        target = (slots[receiver][panel], receiver)
        tags[panel].append(target)
        origins[receiver][target[0]] = panel
    halves_of = []
    for half in range(HALVES):
        sends = {device: [] for device in devices}
        passed = {device: {} for device in devices}
        senders = {device: [None] * slot_count for device in devices}
        for receiver, panel, ways in split_flows():
            sender, hops = ways[half]
            if sender not in devices:
                continue
            target = (slots[receiver][panel], receiver)
            senders[receiver][target[0]] = sender
            if sender == panel:
                sends[sender].append(target)
            else:
                step = passed[sender].setdefault(slots[sender][panel], (hops, []))
                step[1].append(target)
        steps = {
            device: sorted((hops, slot, targets) for slot, (hops, targets) in passed[device].items())
            for device in devices
        }
        halves_of.append((sends, steps, senders))
    return devices, slots, slot_count, tags, origins, halves_of


def encoded(target):
    return -1 if target is None else (target[0] * SIDE + target[1][0]) * SIDE + target[1][1]


def picked(me, table):
    value = jnp.int32(table[0])
    for position in range(1, len(table)):
        if table[position] != table[0]:
            value = jnp.where(me == position, jnp.int32(table[position]), value)
    return value


def padded(items, count):
    return list(items) + [None] * (count - len(items))


def transport_kernel(own_ref, tag_ref, held_ref, tags_ref, send_sem, recv_sem, tag_send, tag_recv, own_sem):
    devices, _, slot_count, tags, origins, halves_of = plan()
    group, row, col = lax.axis_index("groups"), lax.axis_index("row"), lax.axis_index("col")
    me = row * SIDE + col
    half_rows = own_ref.shape[0] // HALVES
    chunk = half_rows // CHUNKS

    def table(entry):
        return picked(me, [encoded(entry(d)) for d in devices])

    def listed(items):
        count = max(len(items(d)) for d in devices)
        return [table(lambda d: padded(items(d), count)[k]) for k in range(count)]

    def places(items):
        return [
            table(lambda d: None if items(d)[slot] is None else (0, items(d)[slot]))
            for slot in range(slot_count)
        ]

    tag_codes = listed(lambda d: tags[d])
    origin_codes = places(lambda d: origins[d])
    send_codes, step_slots, step_codes, sender_codes, last = [], [], [], [], []
    for sends, steps, senders in halves_of:
        send_codes.append(listed(lambda d: sends[d]))
        sender_codes.append(places(lambda d: senders[d]))
        step_count = max(len(steps[d]) for d in devices)

        def step_at(d, k):
            return steps[d][k] if k < len(steps[d]) else (0, -1, [])

        step_slots.append(
            [picked(me, [step_at(d, k)[1] for d in devices]) for k in range(step_count)]
        )
        step_codes.append([listed(lambda d: step_at(d, k)[2]) for k in range(step_count)])
        last.append(
            [
                picked(
                    me,
                    [
                        int(senders[d][slot] is not None and slot not in [t[1] for t in steps[d]])
                        for d in devices
                    ],
                )
                for slot in range(slot_count)
            ]
        )

    def place(code):
        return (group, code // SIDE % SIDE, code % SIDE)

    barrier = pltpu.get_barrier_semaphore()
    for codes in [origin_codes] + sender_codes:
        for code in codes[1:]:
            @pl.when(code >= 0)
            def _():
                pl.semaphore_signal(barrier, inc=1, device_id=place(code), device_id_type=MESH)
    receivers = [
        len(tags[d])
        + sum(len(sends[d]) + sum(len(t[2]) for t in steps[d]) for sends, steps, _ in halves_of)
        for d in devices
    ]
    pl.semaphore_wait(barrier, picked(me, receivers))

    own_copy = pltpu.make_async_copy(own_ref, held_ref.at[0], own_sem.at[0])
    own_tag = pltpu.make_async_copy(tag_ref, tags_ref.at[0], own_sem.at[1])

    def tagged(code, index):
        slot = code // (SIDE * SIDE)
        return pltpu.make_async_remote_copy(
            src_ref=tag_ref,
            dst_ref=tags_ref.at[slot],
            send_sem=tag_send.at[index],
            recv_sem=tag_recv.at[slot],
            device_id=place(code),
            device_id_type=MESH,
        )

    def piece(half, q):
        return pl.ds(half * half_rows + q * chunk, chunk)

    def moved(source, slot, code, index, half, q):
        return pltpu.make_async_remote_copy(
            src_ref=source.at[piece(half, q)],
            dst_ref=held_ref.at[slot, piece(half, q)],
            send_sem=send_sem.at[half, index, q],
            recv_sem=recv_sem.at[half, slot, q],
            device_id=place(code),
            device_id_type=MESH,
        )

    def arrived(slot, half, q):
        moved(held_ref.at[slot], slot, me, 0, half, q).wait_recv()

    for index, code in enumerate(tag_codes):
        @pl.when(code >= 0)
        def _():
            tagged(code, index).start()
    own_tag.start()

    def start_own(q, carry):
        for half in range(HALVES):
            for index, code in enumerate(send_codes[half]):
                @pl.when(code >= 0)
                def _():
                    moved(own_ref, code // (SIDE * SIDE), code, index, half, q).start()
        return carry

    lax.fori_loop(0, CHUNKS, start_own, 0)
    own_copy.start()

    def pass_on(q, carry):
        for half in range(HALVES):
            index = len(send_codes[half])
            for slot, codes in zip(step_slots[half], step_codes[half]):
                @pl.when(slot >= 0)
                def _():
                    arrived(slot, half, q)
                for code in codes:
                    @pl.when(code >= 0)
                    def _():
                        target = code // (SIDE * SIDE)
                        moved(held_ref.at[slot], target, code, index, half, q).start()
                    index += 1
        return carry

    lax.fori_loop(0, CHUNKS, pass_on, 0)

    def finish(q, carry):
        for half in range(HALVES):
            for slot in range(1, slot_count):
                @pl.when(last[half][slot] > 0)
                def _():
                    arrived(slot, half, q)
            codes = send_codes[half] + [code for codes in step_codes[half] for code in codes]
            for index, code in enumerate(codes):
                @pl.when(code >= 0)
                def _():
                    moved(own_ref, 0, code, index, half, q).wait_send()
        return carry

    lax.fori_loop(0, CHUNKS, finish, 0)
    for slot in range(1, slot_count):
        @pl.when(origin_codes[slot] >= 0)
        def _():
            tagged(slot * SIDE * SIDE + me, 0).wait_recv()
    for index, code in enumerate(tag_codes):
        @pl.when(code >= 0)
        def _():
            tagged(code, index).wait_send()
    own_tag.wait()
    own_copy.wait()


def transported(own_block, own_tags):
    devices, _, slot_count, tags, _, halves_of = plan()
    copies = 0
    for sends, steps, _ in halves_of:
        fans = [max((len(t[2]) for t in steps[d][k : k + 1]), default=0) for d in devices for k in range(SLOT_LIMIT)]
        per_step = [max(fans[k::SLOT_LIMIT]) for k in range(SLOT_LIMIT)]
        copies = max(copies, max(len(sends[d]) for d in devices) + sum(per_step))
    return pl.pallas_call(
        transport_kernel,
        out_shape=(
            jax.ShapeDtypeStruct((slot_count,) + own_block.shape, own_block.dtype),
            jax.ShapeDtypeStruct((slot_count,) + own_tags.shape, own_tags.dtype),
        ),
        in_specs=[pl.BlockSpec(memory_space=pl.ANY)] * 2,
        out_specs=(pl.BlockSpec(memory_space=pl.ANY),) * 2,
        scratch_shapes=[
            pltpu.SemaphoreType.DMA((HALVES, copies, CHUNKS)),
            pltpu.SemaphoreType.DMA((HALVES, slot_count, CHUNKS)),
            pltpu.SemaphoreType.DMA((max(len(tags[d]) for d in devices),)),
            pltpu.SemaphoreType.DMA((slot_count,)),
            pltpu.SemaphoreType.DMA((2,)),
        ],
        compiler_params=pltpu.CompilerParams(collective_id=0, has_side_effects=True),
        name="transport",
    )(own_block, own_tags)


def halves(block):
    high = block.astype(jnp.bfloat16)
    return high, (block - high.astype(jnp.float32)).astype(jnp.bfloat16)


def product_kernel(size, meta, table, *refs):
    lefts = refs[:STEPS]
    rights = refs[STEPS : 2 * STEPS]
    out_ref = refs[-1]
    col = meta[1]

    def members(turned):
        for member in range(GROUP):
            position = pl.program_id(0) * GROUP + member
            target = table[position]
            left_parts, right_parts = [], []
            for window in range(STEPS):
                between = table[meta[2 + window] * size + position]
                if turned[window]:
                    place, wanted = target - col * size, between
                else:
                    place, wanted = between - lax.rem(col + window, SIDE) * size, target
                matches = table[meta[5 + window] * size + place] == wanted
                left_high, left_low = halves(lefts[window][0, member])
                block = rights[window][0, place]
                block = block.T if turned[window] else block
                right_high, right_low = halves(jnp.where(matches, block, 0.0))
                left_parts += [left_high, left_low, left_high]
                right_parts += [right_high, right_high, right_low]
            out_ref[member] = jnp.dot(
                jnp.concatenate(left_parts, axis=1),
                jnp.concatenate(right_parts, axis=0),
                preferred_element_type=jnp.float32,
            )

    for second in (False, True):
        for third in (False, True):
            @pl.when(jnp.logical_and(meta[9] == int(second), meta[10] == int(third)))
            def _():
                members((False, second, third))


def multiplied(held, meta, table):
    size, width = held.shape[1], held.shape[2]

    def left_spec(window):
        return pl.BlockSpec(
            (1, GROUP, width, width), lambda i, meta, table: (meta[2 + window], i, 0, 0)
        )

    def right_spec(window):
        return pl.BlockSpec(
            (1, size, width, width),
            lambda i, meta, table: (meta[5 + window], 0, 0, 0),
            pipeline_mode=pl.Buffered(1),
        )

    specs = [left_spec(w) for w in range(STEPS)] + [right_spec(w) for w in range(STEPS)]
    return pl.pallas_call(
        functools.partial(product_kernel, size),
        out_shape=jax.ShapeDtypeStruct((size, width, width), jnp.float32),
        grid_spec=pltpu.PrefetchScalarGridSpec(
            num_scalar_prefetch=2,
            grid=(size // GROUP,),
            in_specs=specs,
            out_specs=pl.BlockSpec((GROUP, width, width), lambda i, meta, table: (i, 0, 0)),
        ),
        compiler_params=pltpu.CompilerParams(vmem_limit_bytes=48 * 1024 * 1024),
        name="multiply",
    )(meta, table, *([held] * len(specs)))


def device_meta(row, col):
    devices, slots = plan()[:2]
    rows = []
    for r, c in devices:
        held = slots[(r, c)]
        left = [held[(r, (c + w) % SIDE)] for w in range(STEPS)]
        right, turned = [], []
        for w in range(STEPS):
            k = (c + w) % SIDE
            right.append(held[(k, c)] if (k, c) in held else held[(c, k)])
            turned.append(0 if (k, c) in held else 1)
        rows.append([r, c] + left + right + turned)
    return jnp.asarray(rows, jnp.int32)[row * SIDE + col]


def square_per_device(values, partner):
    size = partner.shape[0]
    meta = device_meta(lax.axis_index("row"), lax.axis_index("col"))
    tags = jnp.broadcast_to(partner[:, 0][None, :], (8, size))
    held, held_tags = transported(values[:, 0], tags)
    return multiplied(held, meta, held_tags[:, 0, :].reshape(-1))[:, None]


def passed_along(value, axis, steps):
    count = lax.axis_size(axis)
    pairs = [(source, (source + steps) % count) for source in range(count)]
    return lax.ppermute(value, axis, pairs)


def spread(value, axis, root):
    mine = lax.axis_index(axis) == root
    return lax.psum(jnp.where(mine, value, jnp.zeros_like(value)), axis)


def per_device(values, partner):
    rows_tile = values.shape[0]
    col_count = lax.axis_size("col")
    range_count = col_count // lax.axis_size("row")
    range_size = rows_tile // range_count
    column = lax.axis_index("col")
    own_block = values[:, 0]
    own_cols = partner[:, 0]
    accumulated = jnp.zeros(own_block.shape, jnp.float32)
    carried_block = own_block
    carried_cols = own_cols
    for window in range(STEPS):
        if window > 0:
            carried_block, carried_cols = passed_along(
                (carried_block, carried_cols), "col", col_count - 1
            )
        target_range = (column + window) % col_count
        source_row = target_range // range_count
        part_index = target_range % range_count
        mine_block = lax.dynamic_slice_in_dim(own_block, part_index * range_size, range_size, 0)
        mine_cols = lax.dynamic_slice_in_dim(own_cols, part_index * range_size, range_size, 0)
        right_block, right_cols = (
            spread(mine_block, "row", source_row),
            spread(mine_cols, "row", source_row),
        )
        offsets = carried_cols - target_range * range_size
        gathered = jnp.take(right_block, offsets, axis=0)
        reached = jnp.take(right_cols, offsets, axis=0)
        product = jnp.einsum(
            "nxy,nyz->nxz",
            carried_block,
            gathered,
            precision=lax.Precision.HIGHEST,
            preferred_element_type=jnp.float32,
        )
        accumulated = accumulated + jnp.where((reached == own_cols)[:, None, None], product, 0.0)
    return accumulated[:, None]


def solution(mesh):
    square = mesh.shape["row"] == SIDE and mesh.shape["col"] == SIDE
    return jax.shard_map(
        square_per_device if square else per_device,
        mesh=mesh,
        in_specs=(P(("groups", "row"), "col", None, None), P(("groups", "row"), "col")),
        out_specs=P(("groups", "row"), "col", None, None),
        check_vma=False,
    )
```
